256 devices in a mesh: ctx: 8 (over z_lo, core), tp: 32 (over z_hi, y, x).
Axes of the slice: x: 4, y: 4, z: 8 (z_hi: 2, z_lo: 4; z = z_hi * 4 + z_lo), core: 2. Of those that a mesh axis runs over, the one named last changes fastest.
Arguments:
- tokens: bfloat16 [4096, 8192], P('ctx', 'tp'), may hold values from -6 to 6
- w_in: bfloat16 [8192, 3, 8192], P('ctx', None, 'tp'), may hold values from -0.0625 to 0.0625
- short_taps: float32 [3, 3, 8192], P(None, None, 'tp'), may hold values from -3 to 3
- decay_rate: float32 [8192, 16], P('tp'), may hold values from 0.00012207031 to 0.05
- residue: float32 [8192, 16], P('tp'), may hold values from -1.5 to 1.5
- skip_gain: float32 [8192], P('tp'), may hold values from -4 to 4
- w_out: bfloat16 [8192, 8192], P(None, 'tp'), may hold values from -0.0625 to 0.0625
Outputs:
- mixed: bfloat16 [4096, 8192], P('ctx', 'tp')
The draws below stay inside these ranges and needn't reach their ends.
All inputs are finite; a program needn't handle non-finite values.
Results may differ from the reference program's by a relative error of at most 0.007.
Values may be sent and summed in bfloat16 or wider, within the bound.
A program may use at most 128 MiB of HBM per device.

```python
import math
import jax
import jax.numpy as jnp
from jax import lax

D = 8192
ORD = 16
SEQ = 4096


def draw_decay_rate(key, part):
    key = jax.random.fold_in(key, 5)
    spread = jax.random.uniform(key, (D, ORD), jnp.float32)
    low = math.log(1.0 / (2 * SEQ))
    high = math.log(1.0 / 20)
    return jnp.exp(low + spread * (high - low)).astype(jnp.float32)


def level_of(own_key, dims, shards, low, top_value):
    def one(dim, shards_of):
        draws = jax.random.uniform(jax.random.fold_in(jax.random.fold_in(own_key, 6), dim), (shards_of,), jnp.float32, low / len(shards), top_value / len(shards))
        return jnp.repeat(jnp.exp(draws), dims[dim] // shards_of).reshape((-1,) + (1,) * (len(dims) - dim - 1))

    loudness = one(*shards[0])
    for cut in shards[1:]:
        loudness = loudness * one(*cut)
    return loudness


def scatter_about(key, dims, deviation, limit, cuts=(), held_as=jnp.bfloat16):
    loudness = level_of(key, dims, cuts, -0.22, 0.18) if cuts else 1.0
    array = jax.random.normal(key, dims, jnp.float32) * deviation * loudness
    return jnp.minimum(jnp.maximum(array, -limit), limit).astype(held_as)


def setup_inputs(seed: int = 0) -> dict:
    splits = jax.random.split(jax.random.key(seed), 8)
    return {
        "tokens": scatter_about(splits[0], (SEQ, D), 1.0, 6.0, ((0, 8), (1, 32))),
        "w_in": scatter_about(splits[1], (D, 3, D), D ** -0.5, 0.0625, ((0, 8), (2, 32))),
        "short_taps": scatter_about(splits[2], (3, 3, D), 1.0, 3.0, ((2, 32),), jnp.float32),
        "decay_rate": draw_decay_rate(jax.random.fold_in(splits[7], 71), 0),
        "residue": scatter_about(splits[4], (D, ORD), 0.25, 1.5, ((0, 32),), jnp.float32),
        "skip_gain": scatter_about(splits[5], (D,), 1.0, 4.0, ((0, 32),), jnp.float32),
        "w_out": scatter_about(splits[6], (D, D), D ** -0.5, 0.0625, ((1, 32),)),
    }


def reference(tokens, w_in, short_taps, decay_rate, residue, skip_gain, w_out):
    proj = jnp.dot(tokens, w_in.reshape(D, 3 * D), preferred_element_type=jnp.float32)
    proj = proj.astype(jnp.bfloat16).reshape(SEQ, 3, D).astype(jnp.float32)
    zero_row = jnp.zeros((1, 3, D), jnp.float32)
    prev_one = jnp.concatenate([zero_row, proj[:-1]], axis=0)
    prev_two = jnp.concatenate([zero_row, zero_row, proj[:-2]], axis=0)
    feat = short_taps[0] * proj + short_taps[1] * prev_one + short_taps[2] * prev_two
    query, keys, values = (feat[:, 0], feat[:, 1], feat[:, 2])
    drive = keys * values
    pole = jnp.exp(-decay_rate)
    weight = residue * jnp.sqrt(1.0 - pole * pole)

    def advance(state, row):
        state = pole * state + row[:, None]
        return (state, lax.optimization_barrier(jnp.sum(weight * state, axis=1)))
    start_state = jnp.zeros((D, ORD), jnp.float32)
    unused, filtered = lax.scan(advance, start_state, drive)
    conv = filtered + skip_gain * drive
    gated = (query * conv).astype(jnp.bfloat16)
    return jnp.dot(gated, w_out, preferred_element_type=jnp.float32).astype(jnp.bfloat16)
```

```python
import functools
import jax
import jax.numpy as jnp
from jax import lax
from jax.experimental import pallas as pl
from jax.experimental.pallas import tpu as pltpu
from jax.sharding import PartitionSpec as P

MESH = pl.DeviceIdType.MESH
BF = jnp.bfloat16
F32 = jnp.float32
SEGS = 8


def place():
    ctx = lax.axis_index("ctx")
    tp = lax.axis_index("tp")
    return tp // 16, ctx // 2, (tp // 4) % 4, tp % 4, ctx % 2


def dev(h, l, y, x, c):
    return (l * 2 + c, h * 16 + y * 4 + x)


def remote(src, dst, send, recv, device):
    return pltpu.make_async_remote_copy(
        src_ref=src, dst_ref=dst, send_sem=send, recv_sem=recv, device_id=device, device_id_type=MESH
    )


class Gather:
    def __init__(self, buf, where, sems):
        self.buf = buf
        self.h, self.l, y, x, self.c = where
        self.a1 = jnp.where(self.c == 0, x, y)
        self.a2 = jnp.where(self.c == 0, y, x)
        self.s1, self.r1, self.s2, self.r2 = sems
        self.half = buf.shape[2] // 2

    def pos(self, d1, d2):
        a1 = (self.a1 + d1 + 4) % 4
        a2 = (self.a2 + d2 + 4) % 4
        return jnp.where(self.c == 0, a2 * 4 + a1, a1 * 4 + a2)

    def at(self, d1, d2):
        a1 = (self.a1 + d1 + 4) % 4
        a2 = (self.a2 + d2 + 4) % 4
        y = jnp.where(self.c == 0, a2, a1)
        x = jnp.where(self.c == 0, a1, a2)
        return dev(self.h, self.l, y, x, self.c)

    def first(self, o, b, d, arriving):
        unit = self.buf.at[b, self.pos(-d if arriving else 0, 0)]
        return remote(unit, unit, self.s1.at[o, d - 1], self.r1.at[o, d - 1], self.at(d, 0))

    def second(self, o, b, d, slot, arriving):
        way = 1 if slot % 2 == 0 else -1
        origin = 0 if slot < 2 else -way
        if arriving:
            origin = origin - way
        unit = self.buf.at[b, self.pos(-d, origin)]
        if slot >= 2:
            unit = unit.at[pl.ds((slot - 2) * self.half, self.half)]
        return remote(unit, unit, self.s2.at[o, d, slot], self.r2.at[o, d, slot], self.at(0, way))

    def start_own(self, o, b):
        for d in (1, 3, 2):
            self.first(o, b, d, False).start()
        self.start_second(o, b, 0)

    def start_second(self, o, b, d):
        for slot in (0, 1):
            self.second(o, b, d, slot, False).start()

    def pass_first(self, o, b):
        for d in (1, 3, 2):
            self.first(o, b, d, True).wait_recv()
            self.start_second(o, b, d)

    def pass_second(self, o, b):
        for d in (0, 1, 3, 2):
            for slot in (0, 1):
                self.second(o, b, d, slot, True).wait_recv()
                self.second(o, b, d, slot + 2, False).start()

    def finish(self, o, b):
        for d in (0, 1, 3, 2):
            for slot in (2, 3):
                self.second(o, b, d, slot, True).wait_recv()

    def wait_sends(self, o, b):
        for d in (1, 3, 2):
            self.first(o, b, d, False).wait_send()
        for d in range(4):
            for slot in range(4):
                self.second(o, b, d, slot, False).wait_send()


def kernel(
    tokens, w_in, taps, decay, residue, skip, w_out, out,
    tok_all, gat_all, w_all, wo, psend, precv, acc, pf, prev, q_s, u_s, y_s, exc, ends, states,
    ps1, pr1, ps2, pr2, ss, rs, ls, es, er,
):
    rows, chans = tokens.shape
    modes = decay.shape[0]
    where = place()
    h, l, y, x, c = where
    half, odd = l // 2, l % 2
    ctx = l * 2 + c
    me = y * 4 + x
    foreign_type = half != h
    z = h * 4 + l

    barrier = pltpu.get_barrier_semaphore()
    partners = []
    for d in range(1, 8):
        zz = (z + d) % 8
        partners.append(dev(zz // 4, zz % 4, y, x, c))
    partners.append(dev(h, l, y, x, 1 - c))
    for d in range(1, 4):
        partners.append(dev(h, l, y, (x + d) % 4, c))
        partners.append(dev(h, l, (y + d) % 4, x, c))
        partners.append(dev(h, (l + d) % 4, y, x, 1 - c))
    for partner in partners:
        pl.semaphore_signal(barrier, inc=1, device_id=partner, device_id_type=MESH)
    pl.semaphore_wait(barrier, len(partners))

    sibling = dev(h, l, y, x, 1 - c)
    across = l + 1 - 2 * odd
    near = dev(h, across, y, x, c)
    mate = dev(h, (l + 2) % 4, y, x, c)
    opposite = dev(1 - h, l, y, x, c)

    to_l = 2 * h + odd
    foreign = tok_all.at[0, me]
    mine = tok_all.at[1, me]
    f0 = remote(tokens, foreign, ss.at[0], rs.at[0], dev(0, to_l, y, x, c))
    f1 = remote(tokens, foreign, ss.at[1], rs.at[0], dev(1, to_l, y, x, c))
    own_far = remote(tokens, mine, ss.at[2], rs.at[1], opposite)
    own_near = pltpu.make_async_copy(tokens, mine, ls.at[0])

    @pl.when(foreign_type)
    def _():
        f0.start()
        f1.start()

    @pl.when(jnp.logical_not(foreign_type))
    def _():
        own_far.start()
        own_near.start()

    mine_q = 2 * odd + c
    near_q = 2 * (1 - odd) + c
    w_near = remote(w_in, w_all.at[mine_q], ss.at[3], rs.at[3], near)
    w_sib = remote(w_in, w_all.at[mine_q], ss.at[4], rs.at[4], sibling)
    w_loc = pltpu.make_async_copy(w_in, w_all.at[mine_q], ls.at[1])
    w_fwd = remote(w_all.at[near_q], w_all.at[near_q], ss.at[5], rs.at[5], sibling)
    wo_loc = pltpu.make_async_copy(w_out, wo, ls.at[2])
    w_near.start()
    w_sib.start()
    w_loc.start()
    wo_loc.start()

    g = Gather(tok_all, where, (ps1.at[0], pr1.at[0], ps2.at[0], pr2.at[0]))
    f0.wait_recv()
    g.start_own(0, 0)
    g.pass_first(0, 0)

    @pl.when(foreign_type)
    def _():
        own_far.wait_recv()

    @pl.when(jnp.logical_not(foreign_type))
    def _():
        own_near.wait()

    g.start_own(1, 1)
    g.pass_second(0, 0)
    remote(w_in, w_all.at[near_q], ss.at[3], rs.at[3], near).wait_recv()
    w_fwd.start()
    g.pass_first(1, 1)
    g.finish(0, 0)
    w_loc.wait()
    remote(w_in, w_all.at[2 * odd + 1 - c], ss.at[4], rs.at[4], sibling).wait_recv()
    remote(w_in, w_all.at[2 * (1 - odd) + 1 - c], ss.at[5], rs.at[5], sibling).wait_recv()

    def multiply(b, n):
        cols = pl.ds(pl.multiple_of(n * chans, chans), chans)
        total = jnp.zeros((rows, chans), F32)
        for pos in range(16):
            block = w_all[pos // 4, pl.ds((pos % 4) * chans, chans), cols]
            total = total + jnp.dot(tok_all[b, pos], block, preferred_element_type=F32)
        return cols, total

    @pl.loop(0, 3)
    def _(n):
        cols, total = multiply(0, n)
        psend[:, cols] = total.astype(BF)

    part = remote(psend, precv, ss.at[6], rs.at[6], mate)
    part.start()
    g.pass_second(1, 1)
    g.finish(1, 1)

    @pl.loop(0, 3)
    def _(n):
        cols, total = multiply(1, n)
        acc[:, cols] = total

    part.wait_recv()
    BLK = 64

    @pl.loop(0, rows // BLK)
    def _(i):
        r = pl.ds(pl.multiple_of(i * BLK, BLK), BLK)
        total = acc[r, :] + precv[r, :].astype(F32)
        pf[pl.ds(pl.multiple_of(i * BLK + 8, 8), BLK), :] = total.astype(BF).astype(F32)

    prev[0] = pf[pl.ds(rows - 8, 16), :].astype(BF)
    later = ctx + 1
    tail = remote(prev.at[0], prev.at[1], ss.at[7], rs.at[7], dev(h, (later // 2) % 4, y, x, later % 2))

    @pl.when(ctx < 7)
    def _():
        tail.start()

    @pl.when(ctx > 0)
    def _():
        tail.wait_recv()
        pf[0:8, :] = prev[1].astype(F32)[8:16]

    @pl.when(ctx == 0)
    def _():
        pf[0:8, :] = jnp.zeros((8, 3 * chans), F32)

    @pl.loop(0, rows // BLK)
    def _(i):
        feats = []
        for s in range(3):
            feat = None
            block = pf[pl.ds(pl.multiple_of(i * BLK, BLK), BLK + 8), pl.ds(s * chans, chans)]
            for k in range(3):
                piece = block[8 - k : 8 - k + BLK]
                term = taps[k, pl.ds(s, 1), :] * piece
                feat = term if feat is None else feat + term
            feats.append(feat)
        r = pl.ds(pl.multiple_of(i * BLK, BLK), BLK)
        q_s[r, :] = feats[0]
        drive = feats[1] * feats[2]
        for lanes in range(chans // 128):
            u_s[lanes, r, :] = drive[:, lanes * 128 : lanes * 128 + 128]

    seg = rows // SEGS
    index = lax.broadcasted_iota(jnp.int32, (SEGS, 128), 0)

    for lanes in range(chans // 128):
        at = pl.ds(lanes * 128, 128)
        rate = [decay[pl.ds(r, 1), at] for r in range(modes)]
        pole = [jnp.broadcast_to(jnp.exp(-d), (SEGS, 128)) for d in rate]

        def grow(step, state):
            row = u_s[lanes, pl.ds(step, SEGS, stride=seg), :]
            return tuple(p * s + row for p, s in zip(pole, state))

        state = lax.fori_loop(0, seg, grow, tuple(jnp.zeros((SEGS, 128), F32) for _ in range(modes)), unroll=2)
        for r in range(modes):
            value = state[r]
            for k in (1, 2, 4):
                moved = jnp.where(index >= k, pltpu.roll(value, k, 0), 0.0)
                value = value + jnp.exp(-(seg * k) * rate[r]) * moved
            ends[pl.ds(r, 1), at] = value[SEGS - 1 : SEGS]
            exc[r, :, at] = jnp.where(index >= 1, pltpu.roll(value, 1, 0), 0.0)

    for d in range(1, 8):
        @pl.when(ctx + d < 8)
        def _():
            to = ctx + d
            remote(ends, states.at[ctx], es.at[d - 1], er.at[d - 1], dev(h, (to // 2) % 4, y, x, to % 2)).start()

    for d in range(1, 8):
        @pl.when(ctx - d >= 0)
        def _():
            remote(ends, states.at[(ctx - d + 8) % 8], es.at[d - 1], er.at[d - 1], sibling).wait_recv()

    group = jnp.exp(-float(rows) * decay[...])
    coming = lax.fori_loop(
        0, ctx, lambda j, value: group * value + states[j], jnp.zeros((modes, chans), F32)
    )
    ends_in = coming

    for lanes in range(chans // 128):
        at = pl.ds(lanes * 128, 128)
        rate = [decay[pl.ds(r, 1), at] for r in range(modes)]
        pole = [jnp.broadcast_to(jnp.exp(-d), (SEGS, 128)) for d in rate]
        weight = []
        state = []
        for r in range(modes):
            single = jnp.exp(-rate[r])
            weight.append(jnp.broadcast_to(residue[pl.ds(r, 1), at] * jnp.sqrt(1.0 - single * single), (SEGS, 128)))
            lead = jnp.exp(-rate[r] * (index * seg).astype(F32))
            state.append(exc[r, :, at] + lead * ends_in[r : r + 1, lanes * 128 : lanes * 128 + 128])

        def emit(step, state):
            row = u_s[lanes, pl.ds(step, SEGS, stride=seg), :]
            state = tuple(p * s + row for p, s in zip(pole, state))
            terms = [w * s for w, s in zip(weight, state)]
            while len(terms) > 1:
                terms = [a + b for a, b in zip(terms[0::2], terms[1::2])]
            y_s[lanes, pl.ds(step, SEGS, stride=seg), :] = terms[0]
            return state

        lax.fori_loop(0, seg, emit, tuple(state), unroll=2)

    @pl.loop(0, rows // BLK)
    def _(i):
        r = pl.ds(pl.multiple_of(i * BLK, BLK), BLK)
        for lanes in range(chans // 128):
            at = pl.ds(lanes * 128, 128)
            conv = y_s[lanes, r, :] + skip[:, at] * u_s[lanes, r, :]
            gat_all[h, me, r, at] = (q_s[r, at] * conv).astype(BF)

    g2 = Gather(gat_all, where, (ps1.at[1], pr1.at[1], ps2.at[1], pr2.at[1]))
    mine_g = gat_all.at[h, me]
    other_g = gat_all.at[1 - h, me]
    swap = remote(mine_g, mine_g, ss.at[8], rs.at[8], opposite)
    swap.start()
    g2.start_own(0, h)
    g2.pass_first(0, h)
    g2.pass_second(0, h)
    remote(other_g, other_g, ss.at[8], rs.at[8], opposite).wait_recv()
    g2.start_own(1, 1 - h)
    g2.finish(0, h)
    wo_loc.wait()

    def project(b):
        total = jnp.zeros((rows, chans), F32)
        for pos in range(16):
            block = wo[pl.ds(pl.multiple_of(b * 16 * chans + pos * chans, chans), chans), :]
            total = total + jnp.dot(gat_all[b, pos], block, preferred_element_type=F32)
        return total

    g2.pass_first(1, 1 - h)
    acc[:, 0:chans] = project(h)
    g2.pass_second(1, 1 - h)
    g2.finish(1, 1 - h)
    out[...] = (acc[:, 0:chans] + project(1 - h)).astype(BF)

    @pl.when(foreign_type)
    def _():
        f0.wait_send()
        f1.wait_send()

    @pl.when(jnp.logical_not(foreign_type))
    def _():
        own_far.wait_send()

    w_near.wait_send()
    w_sib.wait_send()
    w_fwd.wait_send()
    part.wait_send()
    swap.wait_send()

    @pl.when(ctx < 7)
    def _():
        tail.wait_send()

    for d in range(1, 8):
        @pl.when(ctx + d < 8)
        def _():
            remote(ends, states.at[ctx], es.at[d - 1], er.at[d - 1], sibling).wait_send()

    for o in range(2):
        g.wait_sends(o, o)
    g2.wait_sends(0, h)
    g2.wait_sends(1, 1 - h)


def body(tokens, w_in, short_taps, decay_rate, residue, skip_gain, w_out):
    rows, chans = tokens.shape
    depth = w_in.shape[0]
    modes = decay_rate.shape[1]
    vmem = pl.BlockSpec(memory_space=pltpu.VMEM)
    any_ = pl.BlockSpec(memory_space=pl.ANY)
    dma = pltpu.SemaphoreType.DMA
    return pl.pallas_call(
        kernel,
        out_shape=jax.ShapeDtypeStruct((rows, chans), BF),
        in_specs=[vmem, any_, vmem, vmem, vmem, vmem, any_],
        out_specs=vmem,
        scratch_shapes=[
            pltpu.VMEM((2, 16, rows, chans), BF),
            pltpu.VMEM((2, 16, rows, chans), BF),
            pltpu.VMEM((4, depth, 3 * chans), BF),
            pltpu.VMEM(w_out.shape, BF),
            pltpu.VMEM((rows, 3 * chans), BF),
            pltpu.VMEM((rows, 3 * chans), BF),
            pltpu.VMEM((rows, 3 * chans), F32),
            pltpu.VMEM((rows + 8, 3 * chans), F32),
            pltpu.VMEM((2, 16, 3 * chans), BF),
            pltpu.VMEM((rows, chans), F32),
            pltpu.VMEM((chans // 128, rows, 128), F32),
            pltpu.VMEM((chans // 128, rows, 128), F32),
            pltpu.VMEM((modes, SEGS, chans), F32),
            pltpu.VMEM((modes, chans), F32),
            pltpu.VMEM((8, modes, chans), F32),
            dma((2, 2, 3)),
            dma((2, 2, 3)),
            dma((2, 2, 4, 4)),
            dma((2, 2, 4, 4)),
            dma((9,)),
            dma((9,)),
            dma((3,)),
            dma((7,)),
            dma((7,)),
        ],
        compiler_params=pltpu.CompilerParams(collective_id=0, has_side_effects=True, vmem_limit_bytes=56 << 20),
        name="hyena",
    )(
        tokens, w_in.reshape(depth, 3 * chans), short_taps, decay_rate.T, residue.T,
        skip_gain.reshape(1, chans), w_out,
    )


def solution(mesh):
    in_specs = (
        P("ctx", "tp"),
        P("ctx", None, "tp"),
        P(None, None, "tp"),
        P("tp", None),
        P("tp", None),
        P("tp"),
        P(None, "tp"),
    )
    return jax.shard_map(body, mesh=mesh, in_specs=in_specs, out_specs=P("ctx", "tp"), check_vma=False)
```

```python
import functools
import jax
import jax.numpy as jnp
from jax import lax
from jax.experimental import pallas as pl
from jax.experimental.pallas import tpu as pltpu
from jax.sharding import PartitionSpec as P

MESH = pl.DeviceIdType.MESH
BF = jnp.bfloat16
F32 = jnp.float32
SEGS = 8
LANES = 128
HALVES = 2


def place():
    ctx = lax.axis_index("ctx")
    tp = lax.axis_index("tp")
    return tp // 16, ctx // 2, (tp // 4) % 4, tp % 4, ctx % 2


def dev(h, l, y, x, c):
    return (l * 2 + c, h * 16 + y * 4 + x)


def remote(src, dst, send, recv, device):
    return pltpu.make_async_remote_copy(
        src_ref=src, dst_ref=dst, send_sem=send, recv_sem=recv, device_id=device, device_id_type=MESH
    )


class Gather:
    def __init__(self, buf, where, sems):
        self.buf = buf
        self.h, self.l, y, x, self.c = where
        self.a1 = jnp.where(self.c == 0, x, y)
        self.a2 = jnp.where(self.c == 0, y, x)
        self.s1, self.r1, self.s2, self.r2 = sems
        self.half = buf.shape[2] // 2

    def pos(self, d1, d2):
        a1 = (self.a1 + d1 + 4) % 4
        a2 = (self.a2 + d2 + 4) % 4
        return jnp.where(self.c == 0, a2 * 4 + a1, a1 * 4 + a2)

    def at(self, d1, d2):
        a1 = (self.a1 + d1 + 4) % 4
        a2 = (self.a2 + d2 + 4) % 4
        y = jnp.where(self.c == 0, a2, a1)
        x = jnp.where(self.c == 0, a1, a2)
        return dev(self.h, self.l, y, x, self.c)

    def first(self, o, b, d, arriving):
        unit = self.buf.at[b, self.pos(-d if arriving else 0, 0)]
        return remote(unit, unit, self.s1.at[o, d - 1], self.r1.at[o, d - 1], self.at(d, 0))

    def second(self, o, b, d, slot, arriving):
        way = 1 if slot % 2 == 0 else -1
        origin = 0 if slot < 2 else -way
        if arriving:
            origin = origin - way
        unit = self.buf.at[b, self.pos(-d, origin)]
        if slot >= 2:
            unit = unit.at[pl.ds((slot - 2) * self.half, self.half)]
        return remote(unit, unit, self.s2.at[o, d, slot], self.r2.at[o, d, slot], self.at(0, way))

    def start_own(self, o, b):
        for d in (1, 3, 2):
            self.first(o, b, d, False).start()
        self.start_second(o, b, 0)

    def start_second(self, o, b, d):
        for slot in (0, 1):
            self.second(o, b, d, slot, False).start()

    def pass_first(self, o, b):
        for d in (1, 3, 2):
            self.first(o, b, d, True).wait_recv()
            self.start_second(o, b, d)

    def pass_second(self, o, b):
        for d in (0, 1, 3, 2):
            for slot in (0, 1):
                self.second(o, b, d, slot, True).wait_recv()
                self.second(o, b, d, slot + 2, False).start()

    def finish(self, o, b):
        for d in (0, 1, 3, 2):
            for slot in (2, 3):
                self.second(o, b, d, slot, True).wait_recv()

    def wait_sends(self, o, b):
        for d in (1, 3, 2):
            self.first(o, b, d, False).wait_send()
        for d in range(4):
            for slot in range(4):
                self.second(o, b, d, slot, False).wait_send()


def kernel(
    tokens, w_in, taps, decay, residue, skip, w_out, out,
    tok_all, w_all, wx, gat, psend, precv, acc, acc2, osend, orecv, pf, prev, q_s, u_s, y_s, exc, ends, states,
    ps1, pr1, ps2, pr2, ss, rs, ls, es, er, hs, hr, gs, gr, xs, xr, os, orr,
):
    rows, chans = tokens.shape
    modes = decay.shape[0]
    groups = chans // LANES
    wide = 3 * LANES
    where = place()
    h, l, y, x, c = where
    half, odd = l // 2, l % 2
    ctx = l * 2 + c
    me = y * 4 + x
    foreign_type = half != h
    z = h * 4 + l

    barrier = pltpu.get_barrier_semaphore()
    partners = []
    for d in range(1, 8):
        zz = (z + d) % 8
        partners.append(dev(zz // 4, zz % 4, y, x, c))
    partners.append(dev(h, l, y, x, 1 - c))
    for d in range(1, 4):
        partners.append(dev(h, l, y, (x + d) % 4, c))
        partners.append(dev(h, l, (y + d) % 4, x, c))
        partners.append(dev(h, (l + d) % 4, y, x, 1 - c))
    for partner in partners:
        pl.semaphore_signal(barrier, inc=1, device_id=partner, device_id_type=MESH)

    sibling = dev(h, l, y, x, 1 - c)
    across = l + 1 - 2 * odd
    near = dev(h, across, y, x, c)
    mate = dev(h, (l + 2) % 4, y, x, c)
    opposite = dev(1 - h, l, y, x, c)

    to_l = 2 * h + odd
    foreign = tok_all.at[0, me]
    mine = tok_all.at[1, me]
    f0 = remote(tokens, foreign, ss.at[0], rs.at[0], dev(0, to_l, y, x, c))
    f1 = remote(tokens, foreign, ss.at[1], rs.at[0], dev(1, to_l, y, x, c))
    own_far = remote(tokens, mine, ss.at[2], rs.at[1], opposite)
    own_near = pltpu.make_async_copy(tokens, mine, ls.at[0])

    mine_q = 2 * odd + c
    near_q = 2 * (1 - odd) + c

    def w_piece(g):
        return w_in.at[:, :, pl.ds(g * LANES, LANES)]

    def w_near(g, q):
        return remote(w_piece(g), w_all.at[q, g], hs.at[0, g], hr.at[0, g], near)

    def w_sib(g, q):
        return remote(w_piece(g), w_all.at[q, g], hs.at[1, g], hr.at[1, g], sibling)

    def w_fwd(g, q):
        return remote(w_all.at[q, g], w_all.at[q, g], ss.at[3 + g], rs.at[3 + g], sibling)

    def w_loc(g):
        return pltpu.make_async_copy(w_piece(g), w_all.at[mine_q, g], ls.at[1 + g])

    def o_piece(to_x, g):
        return w_out.at[:, to_x, g]

    o_loc = [pltpu.make_async_copy(o_piece(x, g), wx.at[x, g], ls.at[7 + g]) for g in range(groups)]

    def o_send(d, arriving):
        to_x = (x + d) % 4
        slot = wx.at[(x - d + 4) % 4 if arriving else x, c]
        return remote(o_piece(to_x, c), slot, ss.at[4 + d], rs.at[4 + d], dev(h, l, y, to_x, c))

    def o_fwd(d, arriving):
        slot = wx.at[(x - d + 4) % 4, 1 - c if arriving else c]
        return remote(slot, slot, ss.at[7 + d], rs.at[7 + d], sibling)

    @pl.when(jnp.logical_not(foreign_type))
    def _():
        own_near.start()

    for g in range(groups):
        w_loc(g).start()
    for copy in o_loc:
        copy.start()

    pl.semaphore_wait(barrier, len(partners))

    @pl.when(foreign_type)
    def _():
        f0.start()
        f1.start()

    def start_near(g):
        w_near(g, mine_q).start()

    def pass_near(g):
        w_near(g, near_q).wait_recv()
        w_fwd(g, near_q).start()

    def have_weights(g):
        w_loc(g).wait()
        w_sib(g, 2 * odd + 1 - c).wait_recv()
        w_fwd(g, 2 * (1 - odd) + 1 - c).wait_recv()

    start_near(0)
    for g in range(groups):
        w_sib(g, mine_q).start()

    def multiply(b, g, r):
        total = jnp.zeros((rows // 2, wide), F32)
        for pos in range(16):
            here = pl.ds((pos % 4) * chans, chans)
            block = jnp.concatenate([w_all[pos // 4, g, s, here, :] for s in range(3)], axis=1)
            total = total + jnp.dot(tok_all[b, pos, r, :], block, preferred_element_type=F32)
        return total

    def halves(body):
        @pl.loop(0, 2)
        def _(i):
            body(pl.ds(pl.multiple_of(i * (rows // 2), rows // 2), rows // 2))

    def part(g):
        return remote(psend.at[g], precv.at[g], ss.at[11 + g], rs.at[11 + g], mate)

    def foreign_part(g):
        def tile(r):
            psend[g, r, :] = multiply(0, g, r).astype(BF)

        halves(tile)
        part(g).start()

    def own_part(g):
        def tile(r):
            acc[g, r, :] = multiply(1, g, r)

        halves(tile)

    t = Gather(tok_all, where, (ps1, pr1, ps2, pr2))
    f0.wait_recv()
    t.start_own(0, 0)

    @pl.when(jnp.logical_not(foreign_type))
    def _():
        own_far.start()

    t.pass_first(0, 0)
    start_near(1)
    t.pass_second(0, 0)

    @pl.when(foreign_type)
    def _():
        own_far.wait_recv()

    @pl.when(jnp.logical_not(foreign_type))
    def _():
        own_near.wait()

    t.start_own(1, 1)
    pass_near(0)
    t.finish(0, 0)
    have_weights(0)
    foreign_part(0)
    t.pass_first(1, 1)
    pass_near(1)
    have_weights(1)
    foreign_part(1)
    t.pass_second(1, 1)
    for d in (1, 3, 2):
        o_send(d, False).start()
    t.finish(1, 1)

    BLK = 64
    seg = rows // SEGS
    index = lax.broadcasted_iota(jnp.int32, (SEGS, LANES), 0)
    later = ctx + 1
    before = lax.max(ctx, 1) - 1

    def tail(g):
        return remote(
            prev.at[g, 0], prev.at[g, 1], ss.at[13 + g], rs.at[13 + g], dev(h, (later // 2) % 4, y, x, later % 2)
        )

    def project_rows(g):
        part(g).wait_recv()

        @pl.loop(0, rows // BLK)
        def _(i):
            r = pl.ds(pl.multiple_of(i * BLK, BLK), BLK)
            total = acc[g, r, :] + precv[g, r, :].astype(F32)
            pf[g, pl.ds(pl.multiple_of(i * BLK + 8, 8), BLK), :] = total.astype(BF).astype(F32)

        prev[g, 0] = pf[g, pl.ds(rows - 8, 16), :].astype(BF)

        @pl.when(ctx < 7)
        def _():
            tail(g).start()

    def features(g):
        at = pl.ds(g * LANES, LANES)

        def some(i):
            feats = []
            for s in range(3):
                feat = None
                block = pf[g, pl.ds(pl.multiple_of(i * BLK, BLK), BLK + 8), pl.ds(s * LANES, LANES)]
                for k in range(3):
                    piece = block[8 - k : 8 - k + BLK]
                    term = taps[k, pl.ds(s, 1), at] * piece
                    feat = term if feat is None else feat + term
                feats.append(feat)
            r = pl.ds(pl.multiple_of(i * BLK, BLK), BLK)
            q_s[g, r, :] = feats[0]
            u_s[g, r, :] = feats[1] * feats[2]

        pl.loop(1, rows // BLK)(some)

        @pl.when(ctx > 0)
        def _():
            tail(g).wait_recv()
            pf[g, 0:8, :] = prev[g, 1].astype(F32)[8:16]

        @pl.when(ctx == 0)
        def _():
            pf[g, 0:8, :] = jnp.zeros((8, wide), F32)

        pl.loop(0, 1)(some)

    def rates(g):
        return [decay[pl.ds(r, 1), pl.ds(g * LANES, LANES)] for r in range(modes)]

    def state_copy(g, d, to, slot):
        return remote(ends.at[g], states.at[g, slot], es.at[g, d - 1], er.at[g, d - 1], to)

    def scan_ends(g):
        rate = rates(g)
        pole = [jnp.broadcast_to(jnp.exp(-d), (SEGS, LANES)) for d in rate]

        def grow(step, state):
            row = u_s[g, pl.ds(step, SEGS, stride=seg), :]
            return tuple(p * s + row for p, s in zip(pole, state))

        state = lax.fori_loop(0, seg, grow, tuple(jnp.zeros((SEGS, LANES), F32) for _ in range(modes)), unroll=2)
        for r in range(modes):
            value = state[r]
            for k in (1, 2, 4):
                moved = jnp.where(index >= k, pltpu.roll(value, k, 0), 0.0)
                value = value + jnp.exp(-(seg * k) * rate[r]) * moved
            ends[g, pl.ds(r, 1), :] = value[SEGS - 1 : SEGS]
            exc[g, r] = jnp.where(index >= 1, pltpu.roll(value, 1, 0), 0.0)
        for d in range(1, 8):
            @pl.when(ctx + d < 8)
            def _():
                to = ctx + d
                state_copy(g, d, dev(h, (to // 2) % 4, y, x, to % 2), ctx).start()

    def scan_out(g):
        for d in range(1, 8):
            @pl.when(ctx - d >= 0)
            def _():
                state_copy(g, d, sibling, (ctx - d + 8) % 8).wait_recv()

        group = jnp.exp(-float(rows) * decay[:, pl.ds(g * LANES, LANES)])
        coming = lax.fori_loop(
            0, ctx, lambda j, value: group * value + states[g, j], jnp.zeros((modes, LANES), F32)
        )
        rate = rates(g)
        pole = [jnp.broadcast_to(jnp.exp(-d), (SEGS, LANES)) for d in rate]
        weight = []
        state = []
        for r in range(modes):
            single = jnp.exp(-rate[r])
            scale = residue[pl.ds(r, 1), pl.ds(g * LANES, LANES)] * jnp.sqrt(1.0 - single * single)
            weight.append(jnp.broadcast_to(scale, (SEGS, LANES)))
            lead = jnp.exp(-rate[r] * (index * seg).astype(F32))
            state.append(exc[g, r] + lead * coming[r : r + 1])

        def emit(step, state):
            row = u_s[g, pl.ds(step, SEGS, stride=seg), :]
            state = tuple(p * s + row for p, s in zip(pole, state))
            terms = [w * s for w, s in zip(weight, state)]
            while len(terms) > 1:
                terms = [a + b for a, b in zip(terms[0::2], terms[1::2])]
            y_s[g, pl.ds(step, SEGS, stride=seg), :] = terms[0]
            return state

        lax.fori_loop(0, seg, emit, tuple(state), unroll=2)

        count = rows // BLK // HALVES
        for p in range(HALVES):
            @pl.loop(p * count, (p + 1) * count)
            def _(i):
                r = pl.ds(pl.multiple_of(i * BLK, BLK), BLK)
                conv = y_s[g, r, :] + skip[:, pl.ds(g * LANES, LANES)] * u_s[g, r, :]
                gat[g, y, r, mine_h] = (q_s[g, r, :] * conv).astype(BF)

            swap(g, p, False).start()
            for d in (1, 3, 2):
                along(g, 0, p, d, False).start()

    mine_h = pl.ds(pl.multiple_of(h * LANES, LANES), LANES)
    other_h = pl.ds(pl.multiple_of((1 - h) * LANES, LANES), LANES)
    step = rows // HALVES

    def swap(g, p, arriving):
        unit = gat.at[g, y, pl.ds(p * step, step), other_h if arriving else mine_h]
        return remote(unit, unit, xs.at[g, p], xr.at[g, p], opposite)

    def along(g, o, p, d, arriving):
        from_y = (y - d + 4) % 4 if arriving else y
        unit = gat.at[g, from_y, pl.ds(p * step, step), mine_h if o == 0 else other_h]
        return remote(unit, unit, gs.at[g, o, p, d - 1], gr.at[g, o, p, d - 1], dev(h, l, (y + d) % 4, x, c))

    def pass_gated(g, p):
        swap(g, p, True).wait_recv()
        for d in (1, 3, 2):
            along(g, 1, p, d, False).start()

    def have_gated(g, p):
        for o in range(2):
            for d in (1, 3, 2):
                along(g, o, p, d, True).wait_recv()

    def output(g, to_x, p):
        r = pl.ds(p * step, step)
        total = jnp.zeros((step, chans), F32)
        for k in range(4):
            block = jnp.concatenate([wx[to_x, g, k], wx[to_x, g, 4 + k]], axis=0)
            total = total + jnp.dot(gat[g, k, r, :], block, preferred_element_type=F32)
        return total

    def result(d, p, arriving):
        r = pl.ds(p * step, step)
        return remote(
            osend.at[d - 1, r], orecv.at[d - 1, r], os.at[d - 1, p], orr.at[d - 1, p], dev(h, l, y, (x + d) % 4, c)
        )

    own_part(0)
    project_rows(0)
    own_part(1)
    features(0)
    scan_ends(0)
    scan_out(0)
    project_rows(1)
    features(1)
    scan_ends(1)
    for p in range(HALVES):
        pass_gated(0, p)
    scan_out(1)
    for copy in o_loc:
        copy.wait()
    for d in (1, 3, 2):
        o_send(d, True).wait_recv()
        o_fwd(d, False).start()
    for d in (1, 3, 2):
        o_fwd(d, True).wait_recv()
    for p in range(HALVES):
        have_gated(0, p)
    for p in range(HALVES):
        if p == 1:
            pass_gated(1, 0)
        r = pl.ds(p * step, step)
        for d in range(4):
            acc2[d, r, :] = output(0, (x + d) % 4, p)
    for p in range(1, HALVES):
        pass_gated(1, p)
    for p in range(HALVES):
        r = pl.ds(p * step, step)
        have_gated(1, p)
        for d in (2, 1, 3):
            osend[d - 1, r, :] = (acc2[d, r, :] + output(1, (x + d) % 4, p)).astype(BF)
            result(d, p, False).start()
    for p in range(HALVES):
        r = pl.ds(p * step, step)
        acc2[0, r, :] = acc2[0, r, :] + output(1, x, p)
    for p in range(HALVES):
        r = pl.ds(p * step, step)
        for d in (2, 1, 3):
            result(d, p, True).wait_recv()
        out[r, :] = (
            acc2[0, r, :] + orecv[0, r, :].astype(F32) + orecv[1, r, :].astype(F32) + orecv[2, r, :].astype(F32)
        ).astype(BF)

    @pl.when(foreign_type)
    def _():
        f0.wait_send()
        f1.wait_send()

    @pl.when(jnp.logical_not(foreign_type))
    def _():
        own_far.wait_send()

    for g in range(groups):
        w_near(g, mine_q).wait_send()
        w_sib(g, mine_q).wait_send()
        w_fwd(g, near_q).wait_send()
        part(g).wait_send()
        for p in range(HALVES):
            swap(g, p, False).wait_send()
            for o in range(2):
                for d in (1, 3, 2):
                    along(g, o, p, d, False).wait_send()

        @pl.when(ctx < 7)
        def _():
            tail(g).wait_send()

        for d in range(1, 8):
            @pl.when(ctx + d < 8)
            def _():
                state_copy(g, d, sibling, ctx).wait_send()

    for d in (1, 3, 2):
        o_send(d, False).wait_send()
        o_fwd(d, False).wait_send()
        for p in range(HALVES):
            result(d, p, False).wait_send()
    for o in range(2):
        t.wait_sends(o, o)


def body(tokens, w_in, short_taps, decay_rate, residue, skip_gain, w_out):
    rows, chans = tokens.shape
    depth = w_in.shape[0]
    modes = decay_rate.shape[1]
    groups = chans // LANES
    vmem = pl.BlockSpec(memory_space=pltpu.VMEM)
    any_ = pl.BlockSpec(memory_space=pl.ANY)
    dma = pltpu.SemaphoreType.DMA
    return pl.pallas_call(
        kernel,
        out_shape=jax.ShapeDtypeStruct((rows, chans), BF),
        in_specs=[vmem, any_, vmem, vmem, vmem, vmem, any_],
        out_specs=vmem,
        scratch_shapes=[
            pltpu.VMEM((2, 16, rows, chans), BF),
            pltpu.VMEM((4, groups, 3, depth, LANES), BF),
            pltpu.VMEM((4, groups, 8, LANES, chans), BF),
            pltpu.VMEM((groups, 4, rows, 2 * LANES), BF),
            pltpu.VMEM((groups, rows, 3 * LANES), BF),
            pltpu.VMEM((groups, rows, 3 * LANES), BF),
            pltpu.VMEM((groups, rows, 3 * LANES), F32),
            pltpu.VMEM((4, rows, chans), F32),
            pltpu.VMEM((3, rows, chans), BF),
            pltpu.VMEM((3, rows, chans), BF),
            pltpu.VMEM((groups, rows + 8, 3 * LANES), F32),
            pltpu.VMEM((groups, 2, 16, 3 * LANES), BF),
            pltpu.VMEM((groups, rows, LANES), F32),
            pltpu.VMEM((groups, rows, LANES), F32),
            pltpu.VMEM((groups, rows, LANES), F32),
            pltpu.VMEM((groups, modes, SEGS, LANES), F32),
            pltpu.VMEM((groups, modes, LANES), F32),
            pltpu.VMEM((groups, 8, modes, LANES), F32),
            dma((2, 3)),
            dma((2, 3)),
            dma((2, 4, 4)),
            dma((2, 4, 4)),
            dma((21,)),
            dma((21,)),
            dma((9,)),
            dma((groups, 7)),
            dma((groups, 7)),
            dma((2, groups)),
            dma((2, groups)),
            dma((groups, 2, HALVES, 3)),
            dma((groups, 2, HALVES, 3)),
            dma((groups, HALVES)),
            dma((groups, HALVES)),
            dma((3, HALVES)),
            dma((3, HALVES)),
        ],
        compiler_params=pltpu.CompilerParams(collective_id=0, has_side_effects=True, vmem_limit_bytes=56 << 20),
        name="hyena",
    )(
        tokens, jnp.transpose(w_in, (1, 0, 2)), short_taps, decay_rate.T, residue.T,
        skip_gain.reshape(1, chans), w_out.reshape(8, 4, groups, LANES, chans),
    )


def solution(mesh):
    in_specs = (
        P("ctx", "tp"),
        P("ctx", None, "tp"),
        P(None, None, "tp"),
        P("tp", None),
        P("tp", None),
        P("tp"),
        P(None, "tp"),
    )
    return jax.shard_map(body, mesh=mesh, in_specs=in_specs, out_specs=P("ctx", "tp"), check_vma=False)
```

```python
import functools
import jax
import jax.numpy as jnp
from jax import lax
from jax.experimental import pallas as pl
from jax.experimental.pallas import tpu as pltpu
from jax.sharding import PartitionSpec as P

MESH = pl.DeviceIdType.MESH
BF = jnp.bfloat16
F32 = jnp.float32
SEGS = 8
LANES = 128
HALVES = 2


def place():
    ctx = lax.axis_index("ctx")
    tp = lax.axis_index("tp")
    return tp // 16, ctx // 2, (tp // 4) % 4, tp % 4, ctx % 2


def dev(h, l, y, x, c):
    return (l * 2 + c, h * 16 + y * 4 + x)


def remote(src, dst, send, recv, device):
    return pltpu.make_async_remote_copy(
        src_ref=src, dst_ref=dst, send_sem=send, recv_sem=recv, device_id=device, device_id_type=MESH
    )


class Gather:
    def __init__(self, buf, where, sems):
        self.buf = buf
        self.h, self.l, y, x, self.c = where
        self.a1 = jnp.where(self.c == 0, x, y)
        self.a2 = jnp.where(self.c == 0, y, x)
        self.s1, self.r1, self.s2, self.r2 = sems
        self.step = buf.shape[2] // HALVES

    def unit(self, o, d1, d2, quarter=None):
        a1 = (self.a1 + d1 + 4) % 4
        a2 = (self.a2 + d2 + 4) % 4
        pos = jnp.where(self.c == 0, a2 * 4 + a1, a1 * 4 + a2)
        if quarter is None:
            rows = pl.ds((o % HALVES) * self.step, self.step)
        else:
            rows = pl.ds((o % HALVES) * self.step + quarter * (self.step // 2), self.step // 2)
        return self.buf.at[o // HALVES, pos, rows]

    def at(self, d1, d2):
        a1 = (self.a1 + d1 + 4) % 4
        a2 = (self.a2 + d2 + 4) % 4
        y = jnp.where(self.c == 0, a2, a1)
        x = jnp.where(self.c == 0, a1, a2)
        return dev(self.h, self.l, y, x, self.c)

    def first(self, o, d, arriving):
        unit = self.unit(o, -d if arriving else 0, 0)
        return remote(unit, unit, self.s1.at[o, d - 1], self.r1.at[o, d - 1], self.at(d, 0))

    def second(self, o, d, slot, arriving):
        way = 1 if slot % 2 == 0 else -1
        origin = 0 if slot < 2 else -way
        if arriving:
            origin = origin - way
        unit = self.unit(o, -d, origin, None if slot < 2 else slot - 2)
        return remote(unit, unit, self.s2.at[o, d, slot], self.r2.at[o, d, slot], self.at(0, way))

    def start_own(self, o):
        for d in (1, 3, 2):
            self.first(o, d, False).start()
        self.start_second(o, 0)

    def start_second(self, o, d):
        for slot in (0, 1):
            self.second(o, d, slot, False).start()

    def pass_first(self, o):
        for d in (1, 3, 2):
            self.first(o, d, True).wait_recv()
            self.start_second(o, d)

    def pass_second(self, o):
        for d in (0, 1, 3, 2):
            for slot in (0, 1):
                self.second(o, d, slot, True).wait_recv()
                self.second(o, d, slot + 2, False).start()

    def finish(self, o):
        for d in (0, 1, 3, 2):
            for slot in (2, 3):
                self.second(o, d, slot, True).wait_recv()

    def wait_sends(self, o):
        for d in (1, 3, 2):
            self.first(o, d, False).wait_send()
        for d in range(4):
            for slot in range(4):
                self.second(o, d, slot, False).wait_send()


def kernel(
    tokens, w_in, taps, decay, residue, skip, w_out, out,
    tok_all, w_all, wx, gat, psend, precv, acc, acc2, osend, orecv, pf, prev, q_s, u_s, y_s, exc, ends, states,
    ps1, pr1, ps2, pr2, ss, rs, ls, es, er, hs, hr, gs, gr, xs, xr, os, orr, fs, fr, qs, qr,
):
    rows, chans = tokens.shape
    modes = decay.shape[0]
    groups = chans // LANES
    wide = 3 * LANES
    where = place()
    h, l, y, x, c = where
    half, odd = l // 2, l % 2
    ctx = l * 2 + c
    me = y * 4 + x
    foreign_type = half != h
    z = h * 4 + l

    barrier = pltpu.get_barrier_semaphore()
    partners = []
    for d in range(1, 8):
        zz = (z + d) % 8
        partners.append(dev(zz // 4, zz % 4, y, x, c))
    partners.append(dev(h, l, y, x, 1 - c))
    for d in range(1, 4):
        partners.append(dev(h, l, y, (x + d) % 4, c))
        partners.append(dev(h, l, (y + d) % 4, x, c))
        partners.append(dev(h, (l + d) % 4, y, x, 1 - c))
    for partner in partners:
        pl.semaphore_signal(barrier, inc=1, device_id=partner, device_id_type=MESH)

    sibling = dev(h, l, y, x, 1 - c)
    across = l + 1 - 2 * odd
    near = dev(h, across, y, x, c)
    mate = dev(h, (l + 2) % 4, y, x, c)
    opposite = dev(1 - h, l, y, x, c)

    to_l = 2 * h + odd
    step = rows // HALVES

    def token_copy(kind, p):
        r = pl.ds(p * step, step)
        place = tok_all.at[0 if kind < 2 else 1, me, r]
        to = opposite if kind == 2 else dev(kind, to_l, y, x, c)
        return remote(tokens.at[r], place, fs.at[kind, p], fr.at[kind // 2, p], to)

    own_near = pltpu.make_async_copy(tokens, tok_all.at[1, me], ls.at[0])

    mine_q = 2 * odd + c
    near_q = 2 * (1 - odd) + c

    def w_piece(g):
        return w_in.at[:, :, pl.ds(g * LANES, LANES)]

    def w_near(g, q):
        return remote(w_piece(g), w_all.at[q, g], hs.at[0, g], hr.at[0, g], near)

    def w_sib(g, q):
        return remote(w_piece(g), w_all.at[q, g], hs.at[1, g], hr.at[1, g], sibling)

    def w_fwd(g, q):
        return remote(w_all.at[q, g], w_all.at[q, g], ss.at[3 + g], rs.at[3 + g], sibling)

    def w_loc(g):
        return pltpu.make_async_copy(w_piece(g), w_all.at[mine_q, g], ls.at[1 + g])

    def o_piece(to_x, g):
        return w_out.at[:, to_x, g]

    o_loc = [pltpu.make_async_copy(o_piece(x, g), wx.at[x, g], ls.at[7 + g]) for g in range(groups)]

    def o_send(d, arriving):
        to_x = (x + d) % 4
        slot = wx.at[(x - d + 4) % 4 if arriving else x, c]
        return remote(o_piece(to_x, c), slot, ss.at[4 + d], rs.at[4 + d], dev(h, l, y, to_x, c))

    def o_fwd(d, arriving):
        slot = wx.at[(x - d + 4) % 4, 1 - c if arriving else c]
        return remote(slot, slot, ss.at[7 + d], rs.at[7 + d], sibling)

    @pl.when(jnp.logical_not(foreign_type))
    def _():
        own_near.start()

    for g in range(groups):
        w_loc(g).start()
    for copy in o_loc:
        copy.start()

    pl.semaphore_wait(barrier, len(partners))

    @pl.when(foreign_type)
    def _():
        for p in range(HALVES):
            token_copy(0, p).start()
            token_copy(1, p).start()

    def start_near(g):
        w_near(g, mine_q).start()

    def pass_near(g):
        w_near(g, near_q).wait_recv()
        w_fwd(g, near_q).start()

    def have_weights(g):
        w_loc(g).wait()
        w_sib(g, 2 * odd + 1 - c).wait_recv()
        w_fwd(g, 2 * (1 - odd) + 1 - c).wait_recv()

    start_near(0)
    for g in range(groups):
        w_sib(g, mine_q).start()

    def multiply(b, g, p):
        r = pl.ds(p * step, step)
        total = jnp.zeros((step, wide), F32)
        for pos in range(16):
            here = pl.ds((pos % 4) * chans, chans)
            block = jnp.concatenate([w_all[pos // 4, g, s, here, :] for s in range(3)], axis=1)
            total = total + jnp.dot(tok_all[b, pos, r, :], block, preferred_element_type=F32)
        return total

    def part(g, p):
        r = pl.ds(p * step, step)
        return remote(psend.at[g, r], precv.at[g, r], qs.at[g, p], qr.at[g, p], mate)

    def foreign_part(g, p):
        psend[g, pl.ds(p * step, step), :] = multiply(0, g, p).astype(BF)
        part(g, p).start()

    def own_part(g, p):
        acc[g, pl.ds(p * step, step), :] = multiply(1, g, p)

    def have_own():
        @pl.when(foreign_type)
        def _():
            for p in range(HALVES):
                token_copy(2, p).wait_recv()

        @pl.when(jnp.logical_not(foreign_type))
        def _():
            own_near.wait()

    t = Gather(tok_all, where, (ps1, pr1, ps2, pr2))
    token_copy(0, 0).wait_recv()
    t.start_own(0)
    token_copy(0, 1).wait_recv()

    @pl.when(jnp.logical_not(foreign_type))
    def _():
        for p in range(HALVES):
            token_copy(2, p).start()

    t.pass_first(0)
    t.start_own(1)
    t.pass_second(0)
    start_near(1)
    t.pass_first(1)
    t.finish(0)
    pass_near(0)
    t.pass_second(1)
    have_own()
    t.start_own(2)
    have_weights(0)
    foreign_part(0, 0)
    t.finish(1)
    foreign_part(0, 1)
    t.pass_first(2)
    t.start_own(3)
    t.pass_second(2)
    t.pass_first(3)
    pass_near(1)
    have_weights(1)
    foreign_part(1, 0)
    foreign_part(1, 1)
    t.pass_second(3)
    for d in (1, 3, 2):
        o_send(d, False).start()
    t.finish(2)
    own_part(0, 0)
    own_part(1, 0)
    t.finish(3)
    own_part(0, 1)

    BLK = 64
    seg = rows // SEGS
    index = lax.broadcasted_iota(jnp.int32, (SEGS, LANES), 0)
    later = ctx + 1
    before = lax.max(ctx, 1) - 1

    def tail(g):
        return remote(
            prev.at[g, 0], prev.at[g, 1], ss.at[13 + g], rs.at[13 + g], dev(h, (later // 2) % 4, y, x, later % 2)
        )

    def project_rows(g):
        for p in range(HALVES):
            part(g, p).wait_recv()

        @pl.loop(0, rows // BLK)
        def _(i):
            r = pl.ds(pl.multiple_of(i * BLK, BLK), BLK)
            total = acc[g, r, :] + precv[g, r, :].astype(F32)
            pf[g, pl.ds(pl.multiple_of(i * BLK + 8, 8), BLK), :] = total.astype(BF).astype(F32)

        prev[g, 0] = pf[g, pl.ds(rows - 8, 16), :].astype(BF)

        @pl.when(ctx < 7)
        def _():
            tail(g).start()

    def features(g):
        at = pl.ds(g * LANES, LANES)

        def some(i):
            feats = []
            for s in range(3):
                feat = None
                block = pf[g, pl.ds(pl.multiple_of(i * BLK, BLK), BLK + 8), pl.ds(s * LANES, LANES)]
                for k in range(3):
                    piece = block[8 - k : 8 - k + BLK]
                    term = taps[k, pl.ds(s, 1), at] * piece
                    feat = term if feat is None else feat + term
                feats.append(feat)
            r = pl.ds(pl.multiple_of(i * BLK, BLK), BLK)
            q_s[g, r, :] = feats[0]
            u_s[g, r, :] = feats[1] * feats[2]

        pl.loop(1, rows // BLK)(some)

        @pl.when(ctx > 0)
        def _():
            tail(g).wait_recv()
            pf[g, 0:8, :] = prev[g, 1].astype(F32)[8:16]

        @pl.when(ctx == 0)
        def _():
            pf[g, 0:8, :] = jnp.zeros((8, wide), F32)

        pl.loop(0, 1)(some)

    def rates(g):
        return [decay[pl.ds(r, 1), pl.ds(g * LANES, LANES)] for r in range(modes)]

    def state_copy(g, d, to, slot):
        return remote(ends.at[g], states.at[g, slot], es.at[g, d - 1], er.at[g, d - 1], to)

    def scan_ends(g):
        rate = rates(g)
        pole = [jnp.broadcast_to(jnp.exp(-d), (SEGS, LANES)) for d in rate]

        def grow(step, state):
            row = u_s[g, pl.ds(step, SEGS, stride=seg), :]
            return tuple(p * s + row for p, s in zip(pole, state))

        state = lax.fori_loop(0, seg, grow, tuple(jnp.zeros((SEGS, LANES), F32) for _ in range(modes)), unroll=2)
        for r in range(modes):
            value = state[r]
            for k in (1, 2, 4):
                moved = jnp.where(index >= k, pltpu.roll(value, k, 0), 0.0)
                value = value + jnp.exp(-(seg * k) * rate[r]) * moved
            ends[g, pl.ds(r, 1), :] = value[SEGS - 1 : SEGS]
            exc[g, r] = jnp.where(index >= 1, pltpu.roll(value, 1, 0), 0.0)
        for d in range(1, 8):
            @pl.when(ctx + d < 8)
            def _():
                to = ctx + d
                state_copy(g, d, dev(h, (to // 2) % 4, y, x, to % 2), ctx).start()

    def scan_out(g):
        for d in range(1, 8):
            @pl.when(ctx - d >= 0)
            def _():
                state_copy(g, d, sibling, (ctx - d + 8) % 8).wait_recv()

        group = jnp.exp(-float(rows) * decay[:, pl.ds(g * LANES, LANES)])
        coming = lax.fori_loop(
            0, ctx, lambda j, value: group * value + states[g, j], jnp.zeros((modes, LANES), F32)
        )
        rate = rates(g)
        pole = [jnp.broadcast_to(jnp.exp(-d), (SEGS, LANES)) for d in rate]
        weight = []
        state = []
        for r in range(modes):
            single = jnp.exp(-rate[r])
            scale = residue[pl.ds(r, 1), pl.ds(g * LANES, LANES)] * jnp.sqrt(1.0 - single * single)
            weight.append(jnp.broadcast_to(scale, (SEGS, LANES)))
            lead = jnp.exp(-rate[r] * (index * seg).astype(F32))
            state.append(exc[g, r] + lead * coming[r : r + 1])

        def emit(step, state):
            row = u_s[g, pl.ds(step, SEGS, stride=seg), :]
            state = tuple(p * s + row for p, s in zip(pole, state))
            terms = [w * s for w, s in zip(weight, state)]
            while len(terms) > 1:
                terms = [a + b for a, b in zip(terms[0::2], terms[1::2])]
            y_s[g, pl.ds(step, SEGS, stride=seg), :] = terms[0]
            return state

        lax.fori_loop(0, seg, emit, tuple(state), unroll=2)

        @pl.loop(0, rows // BLK)
        def _(i):
            r = pl.ds(pl.multiple_of(i * BLK, BLK), BLK)
            conv = y_s[g, r, :] + skip[:, pl.ds(g * LANES, LANES)] * u_s[g, r, :]
            gat[g, y, r, mine_h] = (q_s[g, r, :] * conv).astype(BF)

    mine_h = pl.ds(pl.multiple_of(h * LANES, LANES), LANES)
    other_h = pl.ds(pl.multiple_of((1 - h) * LANES, LANES), LANES)
    def swap(g, p, arriving):
        unit = gat.at[g, y, pl.ds(p * step, step), other_h if arriving else mine_h]
        return remote(unit, unit, xs.at[g, p], xr.at[g, p], opposite)

    def along(g, o, p, slot, arriving):
        way = 1 if slot % 2 == 0 else -1
        origin = 0 if slot < 2 else -way
        if arriving:
            origin = origin - way
        if slot < 2:
            r = pl.ds(p * step, step)
        else:
            r = pl.ds(p * step + (slot - 2) * (step // 2), step // 2)
        unit = gat.at[g, (y + origin + 4) % 4, r, mine_h if o == 0 else other_h]
        return remote(unit, unit, gs.at[g, o, p, slot], gr.at[g, o, p, slot], dev(h, l, (y + way + 4) % 4, x, c))

    def send_gated(g, p):
        swap(g, p, False).start()
        for slot in (0, 1):
            along(g, 0, p, slot, False).start()

    def pass_swap(g, p):
        swap(g, p, True).wait_recv()
        for slot in (0, 1):
            along(g, 1, p, slot, False).start()

    def pass_along(g, o, p):
        for slot in (0, 1):
            along(g, o, p, slot, True).wait_recv()
            along(g, o, p, slot + 2, False).start()

    def have_gated(g, p):
        for o in range(2):
            for slot in (2, 3):
                along(g, o, p, slot, True).wait_recv()

    def output(g, to_x, p):
        r = pl.ds(p * step, step)
        total = jnp.zeros((step, chans), F32)
        for k in range(4):
            block = jnp.concatenate([wx[to_x, g, k], wx[to_x, g, 4 + k]], axis=0)
            total = total + jnp.dot(gat[g, k, r, :], block, preferred_element_type=F32)
        return total

    def result(d, p, arriving):
        r = pl.ds(p * step, step)
        return remote(
            osend.at[d - 1, r], orecv.at[d - 1, r], os.at[d - 1, p], orr.at[d - 1, p], dev(h, l, y, (x + d) % 4, c)
        )

    project_rows(0)
    own_part(1, 1)
    project_rows(1)
    features(0)
    scan_ends(0)
    features(1)
    scan_ends(1)
    for o in range(2 * HALVES):
        t.wait_sends(o)
    for copy in o_loc:
        copy.wait()
    scan_out(0)
    send_gated(0, 0)
    scan_out(1)
    send_gated(1, 0)
    send_gated(0, 1)
    send_gated(1, 1)
    pass_along(0, 0, 0)
    pass_along(1, 0, 0)
    pass_along(0, 0, 1)
    pass_swap(0, 0)
    pass_along(1, 0, 1)
    pass_swap(1, 0)
    pass_swap(0, 1)
    pass_swap(1, 1)
    for d in (1, 3, 2):
        o_send(d, True).wait_recv()
        o_fwd(d, False).start()
    pass_along(0, 1, 0)
    pass_along(1, 1, 0)
    pass_along(0, 1, 1)
    for d in (1, 3, 2):
        o_fwd(d, True).wait_recv()
    have_gated(0, 0)
    have_gated(1, 0)

    def send_results(p):
        r = pl.ds(p * step, step)
        for d in (2, 1, 3):
            to_x = (x + d) % 4
            osend[d - 1, r, :] = (output(0, to_x, p) + output(1, to_x, p)).astype(BF)
            result(d, p, False).start()

    send_results(0)
    pass_along(1, 1, 1)
    have_gated(0, 1)
    have_gated(1, 1)
    send_results(1)
    for p in range(HALVES):
        acc2[pl.ds(p * step, step), :] = output(0, x, p) + output(1, x, p)
    for p in range(HALVES):
        r = pl.ds(p * step, step)
        for d in (2, 1, 3):
            result(d, p, True).wait_recv()
        out[r, :] = (
            acc2[r, :] + orecv[0, r, :].astype(F32) + orecv[1, r, :].astype(F32) + orecv[2, r, :].astype(F32)
        ).astype(BF)

    @pl.when(foreign_type)
    def _():
        for p in range(HALVES):
            token_copy(0, p).wait_send()
            token_copy(1, p).wait_send()

    @pl.when(jnp.logical_not(foreign_type))
    def _():
        for p in range(HALVES):
            token_copy(2, p).wait_send()

    for g in range(groups):
        w_near(g, mine_q).wait_send()
        w_sib(g, mine_q).wait_send()
        w_fwd(g, near_q).wait_send()
        for p in range(HALVES):
            part(g, p).wait_send()
            swap(g, p, False).wait_send()
            for o in range(2):
                for slot in range(4):
                    along(g, o, p, slot, False).wait_send()

        @pl.when(ctx < 7)
        def _():
            tail(g).wait_send()

        for d in range(1, 8):
            @pl.when(ctx + d < 8)
            def _():
                state_copy(g, d, sibling, ctx).wait_send()

    for d in (1, 3, 2):
        o_send(d, False).wait_send()
        o_fwd(d, False).wait_send()
        for p in range(HALVES):
            result(d, p, False).wait_send()

def body(tokens, w_in, short_taps, decay_rate, residue, skip_gain, w_out):
    rows, chans = tokens.shape
    depth = w_in.shape[0]
    modes = decay_rate.shape[1]
    groups = chans // LANES
    vmem = pl.BlockSpec(memory_space=pltpu.VMEM)
    any_ = pl.BlockSpec(memory_space=pl.ANY)
    dma = pltpu.SemaphoreType.DMA
    return pl.pallas_call(
        kernel,
        out_shape=jax.ShapeDtypeStruct((rows, chans), BF),
        in_specs=[vmem, any_, vmem, vmem, vmem, vmem, any_],
        out_specs=vmem,
        scratch_shapes=[
            pltpu.VMEM((2, 16, rows, chans), BF),
            pltpu.VMEM((4, groups, 3, depth, LANES), BF),
            pltpu.VMEM((4, groups, 8, LANES, chans), BF),
            pltpu.VMEM((groups, 4, rows, 2 * LANES), BF),
            pltpu.VMEM((groups, rows, 3 * LANES), BF),
            pltpu.VMEM((groups, rows, 3 * LANES), BF),
            pltpu.VMEM((groups, rows, 3 * LANES), F32),
            pltpu.VMEM((rows, chans), F32),
            pltpu.VMEM((3, rows, chans), BF),
            pltpu.VMEM((3, rows, chans), BF),
            pltpu.VMEM((groups, rows + 8, 3 * LANES), F32),
            pltpu.VMEM((groups, 2, 16, 3 * LANES), BF),
            pltpu.VMEM((groups, rows, LANES), F32),
            pltpu.VMEM((groups, rows, LANES), F32),
            pltpu.VMEM((groups, rows, LANES), F32),
            pltpu.VMEM((groups, modes, SEGS, LANES), F32),
            pltpu.VMEM((groups, modes, LANES), F32),
            pltpu.VMEM((groups, 8, modes, LANES), F32),
            dma((2 * HALVES, 3)),
            dma((2 * HALVES, 3)),
            dma((2 * HALVES, 4, 4)),
            dma((2 * HALVES, 4, 4)),
            dma((21,)),
            dma((21,)),
            dma((9,)),
            dma((groups, 7)),
            dma((groups, 7)),
            dma((2, groups)),
            dma((2, groups)),
            dma((groups, 2, HALVES, 4)),
            dma((groups, 2, HALVES, 4)),
            dma((groups, HALVES)),
            dma((groups, HALVES)),
            dma((3, HALVES)),
            dma((3, HALVES)),
            dma((3, HALVES)),
            dma((2, HALVES)),
            dma((groups, HALVES)),
            dma((groups, HALVES)),
        ],
        compiler_params=pltpu.CompilerParams(collective_id=0, has_side_effects=True, vmem_limit_bytes=56 << 20),
        name="hyena",
    )(
        tokens, jnp.transpose(w_in, (1, 0, 2)), short_taps, decay_rate.T, residue.T,
        skip_gain.reshape(1, chans), w_out.reshape(8, 4, groups, LANES, chans),
    )


def solution(mesh):
    in_specs = (
        P("ctx", "tp"),
        P("ctx", None, "tp"),
        P(None, None, "tp"),
        P("tp", None),
        P("tp", None),
        P("tp"),
        P(None, "tp"),
    )
    return jax.shard_map(body, mesh=mesh, in_specs=in_specs, out_specs=P("ctx", "tp"), check_vma=False)
```

```python
import functools
import jax
import jax.numpy as jnp
from jax import lax
from jax.experimental import pallas as pl
from jax.experimental.pallas import tpu as pltpu
from jax.sharding import PartitionSpec as P

MESH = pl.DeviceIdType.MESH
BF = jnp.bfloat16
F32 = jnp.float32
SEGS = 8
LANES = 128
HALVES = 2


def place():
    ctx = lax.axis_index("ctx")
    tp = lax.axis_index("tp")
    return tp // 16, ctx // 2, (tp // 4) % 4, tp % 4, ctx % 2


def dev(h, l, y, x, c):
    return (l * 2 + c, h * 16 + y * 4 + x)


def remote(src, dst, send, recv, device):
    return pltpu.make_async_remote_copy(
        src_ref=src, dst_ref=dst, send_sem=send, recv_sem=recv, device_id=device, device_id_type=MESH
    )


class Gather:
    def __init__(self, buf, where, sems):
        self.buf = buf
        self.h, self.l, y, x, self.c = where
        self.a1 = jnp.where(self.c == 0, x, y)
        self.a2 = jnp.where(self.c == 0, y, x)
        self.s1, self.r1, self.s2, self.r2 = sems
        self.step = buf.shape[2] // HALVES

    def unit(self, o, d1, d2, quarter=None):
        a1 = (self.a1 + d1 + 4) % 4
        a2 = (self.a2 + d2 + 4) % 4
        pos = jnp.where(self.c == 0, a2 * 4 + a1, a1 * 4 + a2)
        if quarter is None:
            rows = pl.ds((o % HALVES) * self.step, self.step)
        else:
            rows = pl.ds((o % HALVES) * self.step + quarter * (self.step // 2), self.step // 2)
        return self.buf.at[o // HALVES, pos, rows]

    def at(self, d1, d2):
        a1 = (self.a1 + d1 + 4) % 4
        a2 = (self.a2 + d2 + 4) % 4
        y = jnp.where(self.c == 0, a2, a1)
        x = jnp.where(self.c == 0, a1, a2)
        return dev(self.h, self.l, y, x, self.c)

    def first(self, o, d, arriving):
        unit = self.unit(o, -d if arriving else 0, 0)
        return remote(unit, unit, self.s1.at[o % 2, d - 1], self.r1.at[o, d - 1], self.at(d, 0))

    def second(self, o, d, slot, arriving):
        way = 1 if slot % 2 == 0 else -1
        origin = 0 if slot < 2 else -way
        if arriving:
            origin = origin - way
        unit = self.unit(o, -d, origin, None if slot < 2 else slot - 2)
        return remote(unit, unit, self.s2.at[o % 2, d, slot], self.r2.at[o, d, slot], self.at(0, way))

    def start_own(self, o):
        for d in (1, 3, 2):
            self.first(o, d, False).start()
        self.start_second(o, 0)

    def start_second(self, o, d):
        for slot in (0, 1):
            self.second(o, d, slot, False).start()

    def pass_first(self, o):
        for d in (1, 3, 2):
            self.first(o, d, True).wait_recv()
            self.start_second(o, d)

    def pass_second(self, o):
        for d in (0, 1, 3, 2):
            for slot in (0, 1):
                self.second(o, d, slot, True).wait_recv()
                self.second(o, d, slot + 2, False).start()

    def finish(self, o):
        for d in (0, 1, 3, 2):
            for slot in (2, 3):
                self.second(o, d, slot, True).wait_recv()

    def wait_sends(self, o):
        for d in (1, 3, 2):
            self.first(o, d, False).wait_send()
        for d in range(4):
            for slot in range(4):
                self.second(o, d, slot, False).wait_send()


def kernel(
    tokens, w_in, taps, decay, residue, skip, w_out, out,
    tok_all, w_all, wx, gat, psend, precv, acc, acc2, osend, orecv, pf, prev, q_s, u_s, y_s, exc, ends, states,
    ps1, pr1, ps2, pr2, ss, rs, ls, es, er, hs, hr, gr, xs, xr, orr, fs, fr, qs, qr, bs, br,
):
    rows, chans = tokens.shape
    modes = decay.shape[0]
    groups = chans // LANES
    wide = 3 * LANES
    where = place()
    h, l, y, x, c = where
    half, odd = l // 2, l % 2
    ctx = l * 2 + c
    me = y * 4 + x
    foreign_type = half != h
    z = h * 4 + l

    barrier = pltpu.get_barrier_semaphore()
    partners = []
    for d in range(1, 8):
        zz = (z + d) % 8
        partners.append(dev(zz // 4, zz % 4, y, x, c))
    partners.append(dev(h, l, y, x, 1 - c))
    for d in range(1, 4):
        partners.append(dev(h, l, y, (x + d) % 4, c))
        partners.append(dev(h, l, (y + d) % 4, x, c))
        partners.append(dev(h, (l + d) % 4, y, x, 1 - c))
    for partner in partners:
        pl.semaphore_signal(barrier, inc=1, device_id=partner, device_id_type=MESH)

    sibling = dev(h, l, y, x, 1 - c)
    across = l + 1 - 2 * odd
    near = dev(h, across, y, x, c)
    mate = dev(h, (l + 2) % 4, y, x, c)
    opposite = dev(1 - h, l, y, x, c)

    to_l = 2 * h + odd
    step = rows // HALVES

    def token_copy(kind, p):
        r = pl.ds(p * step, step)
        place = tok_all.at[0 if kind < 2 else 1, me, r]
        to = opposite if kind == 2 else dev(kind, to_l, y, x, c)
        return remote(tokens.at[r], place, fs.at[kind, p], fr.at[kind // 2, p], to)

    own_near = pltpu.make_async_copy(tokens, tok_all.at[1, me], ls.at[0])

    mine_q = 2 * odd + c
    near_q = 2 * (1 - odd) + c

    def w_piece(g):
        return w_in.at[:, :, pl.ds(g * LANES, LANES)]

    def w_near(g, q):
        return remote(w_piece(g), w_all.at[q, g], hs.at[0, g], hr.at[0, g], near)

    def w_near_b(s, q):
        return remote(w_in.at[s, :, pl.ds(LANES, LANES)], w_all.at[q, 1, s], bs.at[0, s], br.at[0, s], near)

    def w_fwd_b(s, q):
        block = w_all.at[q, 1, s]
        return remote(block, block, bs.at[1, s], br.at[1, s], sibling)

    def w_sib(g, q):
        return remote(w_piece(g), w_all.at[q, g], hs.at[1, g], hr.at[1, g], sibling)

    def w_fwd(g, q):
        return remote(w_all.at[q, g], w_all.at[q, g], ss.at[3 + g], rs.at[3 + g], sibling)

    def w_loc(g):
        return pltpu.make_async_copy(w_piece(g), w_all.at[mine_q, g], ls.at[1 + g])

    def o_piece(to_x, g):
        return w_out.at[:, to_x, g]

    o_loc = [pltpu.make_async_copy(o_piece(x, g), wx.at[x, g], ls.at[7 + g]) for g in range(groups)]

    def o_send(d, arriving):
        to_x = (x + d) % 4
        slot = wx.at[(x - d + 4) % 4 if arriving else x, c]
        return remote(o_piece(to_x, c), slot, ss.at[4 + d], rs.at[4 + d], dev(h, l, y, to_x, c))

    def o_fwd(d, arriving):
        slot = wx.at[(x - d + 4) % 4, 1 - c if arriving else c]
        return remote(slot, slot, ss.at[7 + d], rs.at[7 + d], sibling)

    @pl.when(jnp.logical_not(foreign_type))
    def _():
        own_near.start()

    for g in range(groups):
        w_loc(g).start()
    for copy in o_loc:
        copy.start()

    pl.semaphore_wait(barrier, len(partners))

    @pl.when(foreign_type)
    def _():
        for p in range(HALVES):
            token_copy(0, p).start()
            token_copy(1, p).start()

    def pass_near():
        w_near(0, near_q).wait_recv()
        w_fwd(0, near_q).start()

    def pass_near_b(s):
        w_near_b(s, near_q).wait_recv()
        w_fwd_b(s, near_q).start()

    def have_weights(g):
        w_loc(g).wait()
        w_sib(g, 2 * odd + 1 - c).wait_recv()

    far_q = 2 * (1 - odd) + 1 - c
    w_near(0, mine_q).start()
    for g in range(groups):
        w_sib(g, mine_q).start()

    def multiply(b, g, p):
        r = pl.ds(p * step, step)
        total = jnp.zeros((step, wide), F32)
        for pos in range(16):
            here = pl.ds((pos % 4) * chans, chans)
            block = jnp.concatenate([w_all[pos // 4, g, s, here, :] for s in range(3)], axis=1)
            total = total + jnp.dot(tok_all[b, pos, r, :], block, preferred_element_type=F32)
        return total

    def part(p):
        r = pl.ds(p * step, step)
        return remote(psend.at[0, r], precv.at[0, r], qs.at[p], qr.at[p], mate)

    def foreign_part(p):
        psend[0, pl.ds(p * step, step), :] = multiply(0, 0, p).astype(BF)
        part(p).start()

    def part_b(s):
        cols = pl.ds(s * LANES, LANES)
        return remote(psend.at[1, :, cols], precv.at[1, :, cols], bs.at[2, s], br.at[2, s], mate)

    def foreign_part_b(s):
        w_fwd_b(s, far_q).wait_recv()
        for p in range(HALVES):
            r = pl.ds(p * step, step)
            total = jnp.zeros((step, LANES), F32)
            for pos in range(16):
                block = w_all[pos // 4, 1, s, pl.ds((pos % 4) * chans, chans), :]
                total = total + jnp.dot(tok_all[0, pos, r, :], block, preferred_element_type=F32)
            psend[1, r, pl.ds(s * LANES, LANES)] = total.astype(BF)
        part_b(s).start()

    def own_part(g, p):
        acc[g, pl.ds(p * step, step), :] = multiply(1, g, p)

    def have_own():
        @pl.when(foreign_type)
        def _():
            for p in range(HALVES):
                token_copy(2, p).wait_recv()

        @pl.when(jnp.logical_not(foreign_type))
        def _():
            own_near.wait()

    t = Gather(tok_all, where, (ps1, pr1, ps2, pr2))
    token_copy(0, 0).wait_recv()
    t.start_own(0)
    token_copy(0, 1).wait_recv()

    @pl.when(jnp.logical_not(foreign_type))
    def _():
        for p in range(HALVES):
            token_copy(2, p).start()

    t.pass_first(0)
    t.start_own(1)
    t.pass_second(0)
    w_near_b(0, mine_q).start()
    t.pass_first(1)
    t.finish(0)
    pass_near()
    w_near_b(1, mine_q).start()
    t.pass_second(1)
    have_own()
    t.wait_sends(0)
    t.start_own(2)
    have_weights(0)
    w_fwd(0, far_q).wait_recv()
    foreign_part(0)
    t.finish(1)
    w_near_b(2, mine_q).start()
    foreign_part(1)
    t.pass_first(2)
    t.wait_sends(1)
    t.start_own(3)
    pass_near_b(0)
    t.pass_second(2)
    have_weights(1)
    foreign_part_b(0)
    t.pass_first(3)
    pass_near_b(1)
    foreign_part_b(1)
    t.finish(2)
    own_part(0, 0)
    t.pass_second(3)
    pass_near_b(2)
    foreign_part_b(2)
    for d in (1, 3, 2):
        o_send(d, False).start()
    own_part(1, 0)
    t.finish(3)
    own_part(0, 1)

    BLK = 64
    seg = rows // SEGS
    index = lax.broadcasted_iota(jnp.int32, (SEGS, LANES), 0)
    later = ctx + 1
    before = lax.max(ctx, 1) - 1

    def tail(g):
        return remote(
            prev.at[g, 0], prev.at[g, 1], ss.at[13 + g], rs.at[13 + g], dev(h, (later // 2) % 4, y, x, later % 2)
        )

    def project_rows(g):
        if g == 0:
            for p in range(HALVES):
                part(p).wait_recv()
        else:
            for s in range(3):
                part_b(s).wait_recv()

        @pl.loop(0, rows // BLK)
        def _(i):
            r = pl.ds(pl.multiple_of(i * BLK, BLK), BLK)
            total = acc[g, r, :] + precv[g, r, :].astype(F32)
            pf[g, pl.ds(pl.multiple_of(i * BLK + 8, 8), BLK), :] = total.astype(BF).astype(F32)

        prev[g, 0] = pf[g, pl.ds(rows - 8, 16), :].astype(BF)

        @pl.when(ctx < 7)
        def _():
            tail(g).start()

    def features(g):
        at = pl.ds(g * LANES, LANES)

        def some(i):
            feats = []
            for s in range(3):
                feat = None
                block = pf[g, pl.ds(pl.multiple_of(i * BLK, BLK), BLK + 8), pl.ds(s * LANES, LANES)]
                for k in range(3):
                    piece = block[8 - k : 8 - k + BLK]
                    term = taps[k, pl.ds(s, 1), at] * piece
                    feat = term if feat is None else feat + term
                feats.append(feat)
            r = pl.ds(pl.multiple_of(i * BLK, BLK), BLK)
            q_s[g, r, :] = feats[0]
            u_s[g, r, :] = feats[1] * feats[2]

        pl.loop(1, rows // BLK)(some)

        @pl.when(ctx > 0)
        def _():
            tail(g).wait_recv()
            pf[g, 0:8, :] = prev[g, 1].astype(F32)[8:16]

        @pl.when(ctx == 0)
        def _():
            pf[g, 0:8, :] = jnp.zeros((8, wide), F32)

        pl.loop(0, 1)(some)

    def rates(g):
        return [decay[pl.ds(r, 1), pl.ds(g * LANES, LANES)] for r in range(modes)]

    def state_copy(g, d, to, slot):
        return remote(ends.at[g], states.at[g, slot], es.at[g, d - 1], er.at[g, d - 1], to)

    def scan_ends(g):
        rate = rates(g)
        pole = [jnp.broadcast_to(jnp.exp(-d), (SEGS, LANES)) for d in rate]

        def grow(step, state):
            row = u_s[g, pl.ds(step, SEGS, stride=seg), :]
            return tuple(p * s + row for p, s in zip(pole, state))

        state = lax.fori_loop(0, seg, grow, tuple(jnp.zeros((SEGS, LANES), F32) for _ in range(modes)), unroll=2)
        for r in range(modes):
            value = state[r]
            for k in (1, 2, 4):
                moved = jnp.where(index >= k, pltpu.roll(value, k, 0), 0.0)
                value = value + jnp.exp(-(seg * k) * rate[r]) * moved
            ends[g, pl.ds(r, 1), :] = value[SEGS - 1 : SEGS]
            exc[g, r] = jnp.where(index >= 1, pltpu.roll(value, 1, 0), 0.0)
        for d in range(1, 8):
            @pl.when(ctx + d < 8)
            def _():
                to = ctx + d
                state_copy(g, d, dev(h, (to // 2) % 4, y, x, to % 2), ctx).start()

    def scan_out(g):
        for d in range(1, 8):
            @pl.when(ctx - d >= 0)
            def _():
                state_copy(g, d, sibling, (ctx - d + 8) % 8).wait_recv()

        group = jnp.exp(-float(rows) * decay[:, pl.ds(g * LANES, LANES)])
        coming = lax.fori_loop(
            0, ctx, lambda j, value: group * value + states[g, j], jnp.zeros((modes, LANES), F32)
        )
        rate = rates(g)
        pole = [jnp.broadcast_to(jnp.exp(-d), (SEGS, LANES)) for d in rate]
        weight = []
        state = []
        for r in range(modes):
            single = jnp.exp(-rate[r])
            scale = residue[pl.ds(r, 1), pl.ds(g * LANES, LANES)] * jnp.sqrt(1.0 - single * single)
            weight.append(jnp.broadcast_to(scale, (SEGS, LANES)))
            lead = jnp.exp(-rate[r] * (index * seg).astype(F32))
            state.append(exc[g, r] + lead * coming[r : r + 1])

        def emit(step, state):
            row = u_s[g, pl.ds(step, SEGS, stride=seg), :]
            state = tuple(p * s + row for p, s in zip(pole, state))
            terms = [w * s for w, s in zip(weight, state)]
            while len(terms) > 1:
                terms = [a + b for a, b in zip(terms[0::2], terms[1::2])]
            y_s[g, pl.ds(step, SEGS, stride=seg), :] = terms[0]
            return state

        lax.fori_loop(0, seg, emit, tuple(state), unroll=2)

        @pl.loop(0, rows // BLK)
        def _(i):
            r = pl.ds(pl.multiple_of(i * BLK, BLK), BLK)
            conv = y_s[g, r, :] + skip[:, pl.ds(g * LANES, LANES)] * u_s[g, r, :]
            gat[g, y, r, mine_h] = (q_s[g, r, :] * conv).astype(BF)

    mine_h = pl.ds(pl.multiple_of(h * LANES, LANES), LANES)
    other_h = pl.ds(pl.multiple_of((1 - h) * LANES, LANES), LANES)
    def swap(g, p, arriving):
        unit = gat.at[g, y, pl.ds(p * step, step), other_h if arriving else mine_h]
        return remote(unit, unit, xs.at[g, p], xr.at[g, p], opposite)

    def along(g, o, p, slot, arriving):
        way = 1 if slot % 2 == 0 else -1
        origin = 0 if slot < 2 else -way
        if arriving:
            origin = origin - way
        if slot < 2:
            r = pl.ds(p * step, step)
        else:
            r = pl.ds(p * step + (slot - 2) * (step // 2), step // 2)
        unit = gat.at[g, (y + origin + 4) % 4, r, mine_h if o == 0 else other_h]
        return remote(unit, unit, ps2.at[g, o * 2 + p, slot], gr.at[g, o, p, slot], dev(h, l, (y + way + 4) % 4, x, c))

    def send_gated(g, p):
        swap(g, p, False).start()
        for slot in (0, 1):
            along(g, 0, p, slot, False).start()

    def pass_swap(g, p):
        swap(g, p, True).wait_recv()
        for slot in (0, 1):
            along(g, 1, p, slot, False).start()

    def pass_along(g, o, p):
        for slot in (0, 1):
            along(g, o, p, slot, True).wait_recv()
            along(g, o, p, slot + 2, False).start()

    def have_gated(g, p):
        for o in range(2):
            for slot in (2, 3):
                along(g, o, p, slot, True).wait_recv()

    def output(g, to_x, p):
        r = pl.ds(p * step, step)
        total = jnp.zeros((step, chans), F32)
        for k in range(4):
            block = jnp.concatenate([wx[to_x, g, k], wx[to_x, g, 4 + k]], axis=0)
            total = total + jnp.dot(gat[g, k, r, :], block, preferred_element_type=F32)
        return total

    def result(d, p, arriving):
        r = pl.ds(p * step, step)
        return remote(
            osend.at[d - 1, r], orecv.at[d - 1, r], ps1.at[p, d - 1], orr.at[d - 1, p], dev(h, l, y, (x + d) % 4, c)
        )

    project_rows(0)
    own_part(1, 1)
    project_rows(1)
    features(0)
    scan_ends(0)
    features(1)
    scan_ends(1)
    t.wait_sends(2)
    t.wait_sends(3)
    for copy in o_loc:
        copy.wait()
    scan_out(0)
    send_gated(0, 0)
    scan_out(1)
    send_gated(1, 0)
    send_gated(0, 1)
    send_gated(1, 1)
    pass_along(0, 0, 0)
    pass_along(1, 0, 0)
    pass_along(0, 0, 1)
    pass_swap(0, 0)
    pass_along(1, 0, 1)
    pass_swap(1, 0)
    pass_swap(0, 1)
    pass_swap(1, 1)
    for d in (1, 3, 2):
        o_send(d, True).wait_recv()
        o_fwd(d, False).start()
    pass_along(0, 1, 0)
    pass_along(1, 1, 0)
    pass_along(0, 1, 1)
    pass_along(1, 1, 1)
    for d in (1, 3, 2):
        o_fwd(d, True).wait_recv()
    have_gated(0, 0)
    have_gated(1, 0)

    def send_results(p):
        r = pl.ds(p * step, step)
        for d in (2, 1, 3):
            to_x = (x + d) % 4
            osend[d - 1, r, :] = (output(0, to_x, p) + output(1, to_x, p)).astype(BF)
            result(d, p, False).start()

    send_results(0)
    have_gated(0, 1)
    have_gated(1, 1)
    send_results(1)
    for p in range(HALVES):
        acc2[pl.ds(p * step, step), :] = output(0, x, p) + output(1, x, p)
    for p in range(HALVES):
        r = pl.ds(p * step, step)
        for d in (2, 1, 3):
            result(d, p, True).wait_recv()
        out[r, :] = (
            acc2[r, :] + orecv[0, r, :].astype(F32) + orecv[1, r, :].astype(F32) + orecv[2, r, :].astype(F32)
        ).astype(BF)

    @pl.when(foreign_type)
    def _():
        for p in range(HALVES):
            token_copy(0, p).wait_send()
            token_copy(1, p).wait_send()

    @pl.when(jnp.logical_not(foreign_type))
    def _():
        for p in range(HALVES):
            token_copy(2, p).wait_send()

    for g in range(groups):
        w_sib(g, mine_q).wait_send()
        for p in range(HALVES):
            swap(g, p, False).wait_send()
            for o in range(2):
                for slot in range(4):
                    along(g, o, p, slot, False).wait_send()

        @pl.when(ctx < 7)
        def _():
            tail(g).wait_send()

        for d in range(1, 8):
            @pl.when(ctx + d < 8)
            def _():
                state_copy(g, d, sibling, ctx).wait_send()

    w_near(0, mine_q).wait_send()
    w_fwd(0, near_q).wait_send()
    for p in range(HALVES):
        part(p).wait_send()
    for s in range(3):
        w_near_b(s, mine_q).wait_send()
        w_fwd_b(s, near_q).wait_send()
        part_b(s).wait_send()
    for d in (1, 3, 2):
        o_send(d, False).wait_send()
        o_fwd(d, False).wait_send()
        for p in range(HALVES):
            result(d, p, False).wait_send()

def body(tokens, w_in, short_taps, decay_rate, residue, skip_gain, w_out):
    rows, chans = tokens.shape
    depth = w_in.shape[0]
    modes = decay_rate.shape[1]
    groups = chans // LANES
    vmem = pl.BlockSpec(memory_space=pltpu.VMEM)
    any_ = pl.BlockSpec(memory_space=pl.ANY)
    dma = pltpu.SemaphoreType.DMA
    return pl.pallas_call(
        kernel,
        out_shape=jax.ShapeDtypeStruct((rows, chans), BF),
        in_specs=[vmem, any_, vmem, vmem, vmem, vmem, any_],
        out_specs=vmem,
        scratch_shapes=[
            pltpu.VMEM((2, 16, rows, chans), BF),
            pltpu.VMEM((4, groups, 3, depth, LANES), BF),
            pltpu.VMEM((4, groups, 8, LANES, chans), BF),
            pltpu.VMEM((groups, 4, rows, 2 * LANES), BF),
            pltpu.VMEM((groups, rows, 3 * LANES), BF),
            pltpu.VMEM((groups, rows, 3 * LANES), BF),
            pltpu.VMEM((groups, rows, 3 * LANES), F32),
            pltpu.VMEM((rows, chans), F32),
            pltpu.VMEM((3, rows, chans), BF),
            pltpu.VMEM((3, rows, chans), BF),
            pltpu.VMEM((groups, rows + 8, 3 * LANES), F32),
            pltpu.VMEM((groups, 2, 16, 3 * LANES), BF),
            pltpu.VMEM((groups, rows, LANES), F32),
            pltpu.VMEM((groups, rows, LANES), F32),
            pltpu.VMEM((groups, rows, LANES), F32),
            pltpu.VMEM((groups, modes, SEGS, LANES), F32),
            pltpu.VMEM((groups, modes, LANES), F32),
            pltpu.VMEM((groups, 8, modes, LANES), F32),
            dma((2, 3)),
            dma((2 * HALVES, 3)),
            dma((2, 4, 4)),
            dma((2 * HALVES, 4, 4)),
            dma((21,)),
            dma((21,)),
            dma((9,)),
            dma((groups, 7)),
            dma((groups, 7)),
            dma((2, groups)),
            dma((2, groups)),
            dma((groups, 2, HALVES, 4)),
            dma((groups, HALVES)),
            dma((groups, HALVES)),
            dma((3, HALVES)),
            dma((3, HALVES)),
            dma((2, HALVES)),
            dma((HALVES,)),
            dma((HALVES,)),
            dma((3, 3)),
            dma((3, 3)),
        ],
        compiler_params=pltpu.CompilerParams(collective_id=0, has_side_effects=True, vmem_limit_bytes=56 << 20),
        name="hyena",
    )(
        tokens, jnp.transpose(w_in, (1, 0, 2)), short_taps, decay_rate.T, residue.T,
        skip_gain.reshape(1, chans), w_out.reshape(8, 4, groups, LANES, chans),
    )


def solution(mesh):
    in_specs = (
        P("ctx", "tp"),
        P("ctx", None, "tp"),
        P(None, None, "tp"),
        P("tp", None),
        P("tp", None),
        P("tp"),
        P(None, "tp"),
    )
    return jax.shard_map(body, mesh=mesh, in_specs=in_specs, out_specs=P("ctx", "tp"), check_vma=False)
```

```python
import functools
import jax
import jax.numpy as jnp
from jax import lax
from jax.experimental import pallas as pl
from jax.experimental.pallas import tpu as pltpu
from jax.sharding import PartitionSpec as P

MESH = pl.DeviceIdType.MESH
BF = jnp.bfloat16
F32 = jnp.float32
SEGS = 8
LANES = 128
HALVES = 2


def place():
    ctx = lax.axis_index("ctx")
    tp = lax.axis_index("tp")
    return tp // 16, ctx // 2, (tp // 4) % 4, tp % 4, ctx % 2


def dev(h, l, y, x, c):
    return (l * 2 + c, h * 16 + y * 4 + x)


def remote(src, dst, send, recv, device):
    return pltpu.make_async_remote_copy(
        src_ref=src, dst_ref=dst, send_sem=send, recv_sem=recv, device_id=device, device_id_type=MESH
    )


class Gather:
    def __init__(self, buf, where, sems):
        self.buf = buf
        self.h, self.l, y, x, self.c = where
        self.a1 = jnp.where(self.c == 0, x, y)
        self.a2 = jnp.where(self.c == 0, y, x)
        self.s1, self.r1, self.s2, self.r2 = sems
        self.step = buf.shape[2] // HALVES

    def unit(self, o, d1, d2, quarter=None):
        a1 = (self.a1 + d1 + 4) % 4
        a2 = (self.a2 + d2 + 4) % 4
        pos = jnp.where(self.c == 0, a2 * 4 + a1, a1 * 4 + a2)
        if quarter is None:
            rows = pl.ds((o % HALVES) * self.step, self.step)
        else:
            rows = pl.ds((o % HALVES) * self.step + quarter * (self.step // 2), self.step // 2)
        return self.buf.at[o // HALVES, pos, rows]

    def at(self, d1, d2):
        a1 = (self.a1 + d1 + 4) % 4
        a2 = (self.a2 + d2 + 4) % 4
        y = jnp.where(self.c == 0, a2, a1)
        x = jnp.where(self.c == 0, a1, a2)
        return dev(self.h, self.l, y, x, self.c)

    def first(self, o, d, arriving):
        unit = self.unit(o, -d if arriving else 0, 0)
        return remote(unit, unit, self.s1.at[o % 2, d - 1], self.r1.at[o, d - 1], self.at(d, 0))

    def second(self, o, d, slot, arriving):
        way = 1 if slot % 2 == 0 else -1
        origin = 0 if slot < 2 else -way
        if arriving:
            origin = origin - way
        unit = self.unit(o, -d, origin, None if slot < 2 else slot - 2)
        return remote(unit, unit, self.s2.at[o % 2, d, slot], self.r2.at[o, d, slot], self.at(0, way))

    def start_own(self, o):
        for d in (1, 3, 2):
            self.first(o, d, False).start()
        self.start_second(o, 0)

    def start_second(self, o, d):
        for slot in (0, 1):
            self.second(o, d, slot, False).start()

    def pass_first(self, o):
        for d in (1, 3, 2):
            self.first(o, d, True).wait_recv()
            self.start_second(o, d)

    def pass_second(self, o):
        for d in (0, 1, 3, 2):
            for slot in (0, 1):
                self.second(o, d, slot, True).wait_recv()
                self.second(o, d, slot + 2, False).start()

    def finish(self, o):
        for d in (0, 1, 3, 2):
            for slot in (2, 3):
                self.second(o, d, slot, True).wait_recv()

    def wait_sends(self, o):
        for d in (1, 3, 2):
            self.first(o, d, False).wait_send()
        for d in range(4):
            for slot in range(4):
                self.second(o, d, slot, False).wait_send()


def kernel(
    tokens, w_in, taps, decay, residue, skip, w_out, out,
    tok_all, w_all, wx, gat, psend, precv, acc, acc2, osend, orecv, pf, prev, q_s, u_s, y_s, exc, ends, states,
    ps1, pr1, ps2, pr2, ss, rs, ls, es, er, hs, hr, gr, xs, xr, orr, fs, fr, qs, qr, bs, br,
):
    rows, chans = tokens.shape
    modes = decay.shape[0]
    groups = chans // LANES
    wide = 3 * LANES
    where = place()
    h, l, y, x, c = where
    half, odd = l // 2, l % 2
    ctx = l * 2 + c
    me = y * 4 + x
    foreign_type = half != h
    z = h * 4 + l

    barrier = pltpu.get_barrier_semaphore()
    partners = []
    for d in range(1, 8):
        zz = (z + d) % 8
        partners.append(dev(zz // 4, zz % 4, y, x, c))
    partners.append(dev(h, l, y, x, 1 - c))
    for d in range(1, 4):
        partners.append(dev(h, l, y, (x + d) % 4, c))
        partners.append(dev(h, l, (y + d) % 4, x, c))
        partners.append(dev(h, (l + d) % 4, y, x, 1 - c))
    for partner in partners:
        pl.semaphore_signal(barrier, inc=1, device_id=partner, device_id_type=MESH)

    sibling = dev(h, l, y, x, 1 - c)
    across = l + 1 - 2 * odd
    near = dev(h, across, y, x, c)
    mate = dev(h, (l + 2) % 4, y, x, c)
    opposite = dev(1 - h, l, y, x, c)

    to_l = 2 * h + odd
    step = rows // HALVES

    def token_copy(kind, p):
        r = pl.ds(p * step, step)
        place = tok_all.at[0 if kind < 2 else 1, me, r]
        to = opposite if kind == 2 else dev(kind, to_l, y, x, c)
        return remote(tokens.at[r], place, fs.at[kind, p], fr.at[kind // 2, p], to)

    own_near = pltpu.make_async_copy(tokens, tok_all.at[1, me], ls.at[0])

    mine_q = 2 * odd + c
    near_q = 2 * (1 - odd) + c

    def w_piece(g):
        return w_in.at[:, :, pl.ds(g * LANES, LANES)]

    def w_near(g, q):
        return remote(w_piece(g), w_all.at[q, g], hs.at[0, g], hr.at[0, g], near)

    def w_near_b(s, q):
        return remote(w_in.at[s, :, pl.ds(LANES, LANES)], w_all.at[q, 1, s], bs.at[0, s], br.at[0, s], near)

    def w_fwd_b(s, q):
        block = w_all.at[q, 1, s]
        return remote(block, block, bs.at[1, s], br.at[1, s], sibling)

    def w_sib(g, q):
        return remote(w_piece(g), w_all.at[q, g], hs.at[1, g], hr.at[1, g], sibling)

    def w_fwd(g, q):
        return remote(w_all.at[q, g], w_all.at[q, g], ss.at[3 + g], rs.at[3 + g], sibling)

    def w_loc(g):
        return pltpu.make_async_copy(w_piece(g), w_all.at[mine_q, g], ls.at[1 + g])

    def o_piece(to_x, g):
        return w_out.at[:, to_x, g]

    o_loc = [pltpu.make_async_copy(o_piece(x, g), wx.at[x, g], ls.at[7 + g]) for g in range(groups)]

    def o_send(d, arriving):
        to_x = (x + d) % 4
        slot = wx.at[(x - d + 4) % 4 if arriving else x, c]
        return remote(o_piece(to_x, c), slot, ss.at[4 + d], rs.at[4 + d], dev(h, l, y, to_x, c))

    def o_fwd(d, arriving):
        slot = wx.at[(x - d + 4) % 4, 1 - c if arriving else c]
        return remote(slot, slot, ss.at[7 + d], rs.at[7 + d], sibling)

    @pl.when(jnp.logical_not(foreign_type))
    def _():
        own_near.start()

    for g in range(groups):
        w_loc(g).start()
    for copy in o_loc:
        copy.start()

    pl.semaphore_wait(barrier, len(partners))

    @pl.when(foreign_type)
    def _():
        for p in range(HALVES):
            token_copy(0, p).start()
            token_copy(1, p).start()

    def pass_near():
        w_near(0, near_q).wait_recv()
        w_fwd(0, near_q).start()

    def pass_near_b(s):
        w_near_b(s, near_q).wait_recv()
        w_fwd_b(s, near_q).start()

    def have_weights(g):
        w_loc(g).wait()
        w_sib(g, 2 * odd + 1 - c).wait_recv()

    far_q = 2 * (1 - odd) + 1 - c
    w_near(0, mine_q).start()
    for g in range(groups):
        w_sib(g, mine_q).start()

    def multiply(b, g, p):
        r = pl.ds(p * step, step)
        total = jnp.zeros((step, wide), F32)
        for pos in range(16):
            here = pl.ds((pos % 4) * chans, chans)
            block = jnp.concatenate([w_all[pos // 4, g, s, here, :] for s in range(3)], axis=1)
            total = total + jnp.dot(tok_all[b, pos, r, :], block, preferred_element_type=F32)
        return total

    def part(p):
        r = pl.ds(p * step, step)
        return remote(psend.at[0, r], precv.at[0, r], qs.at[p], qr.at[p], mate)

    def foreign_part(p):
        psend[0, pl.ds(p * step, step), :] = multiply(0, 0, p).astype(BF)
        part(p).start()

    def part_b(s):
        cols = pl.ds(s * LANES, LANES)
        return remote(psend.at[1, :, cols], precv.at[1, :, cols], bs.at[2, s], br.at[2, s], mate)

    def foreign_part_b(s):
        w_fwd_b(s, far_q).wait_recv()
        for p in range(HALVES):
            r = pl.ds(p * step, step)
            total = jnp.zeros((step, LANES), F32)
            for pos in range(16):
                block = w_all[pos // 4, 1, s, pl.ds((pos % 4) * chans, chans), :]
                total = total + jnp.dot(tok_all[0, pos, r, :], block, preferred_element_type=F32)
            psend[1, r, pl.ds(s * LANES, LANES)] = total.astype(BF)
        part_b(s).start()

    def own_part(g, p):
        acc[g, pl.ds(p * step, step), :] = multiply(1, g, p)

    def have_own():
        @pl.when(foreign_type)
        def _():
            for p in range(HALVES):
                token_copy(2, p).wait_recv()

        @pl.when(jnp.logical_not(foreign_type))
        def _():
            own_near.wait()

    t = Gather(tok_all, where, (ps1, pr1, ps2, pr2))
    token_copy(0, 0).wait_recv()
    t.start_own(0)
    token_copy(0, 1).wait_recv()

    @pl.when(jnp.logical_not(foreign_type))
    def _():
        for p in range(HALVES):
            token_copy(2, p).start()

    t.pass_first(0)
    t.start_own(1)
    t.pass_second(0)
    w_near_b(0, mine_q).start()
    t.pass_first(1)
    t.finish(0)
    pass_near()
    w_near_b(1, mine_q).start()
    t.pass_second(1)
    have_own()
    t.wait_sends(0)
    t.start_own(2)
    have_weights(0)
    w_fwd(0, far_q).wait_recv()
    foreign_part(0)
    t.finish(1)
    w_near_b(2, mine_q).start()
    foreign_part(1)
    t.pass_first(2)
    t.wait_sends(1)
    t.start_own(3)
    pass_near_b(0)
    t.pass_second(2)
    have_weights(1)
    foreign_part_b(0)
    t.pass_first(3)
    pass_near_b(1)
    foreign_part_b(1)
    t.pass_second(3)
    pass_near_b(2)
    foreign_part_b(2)
    for d in (1, 3, 2):
        o_send(d, False).start()
    t.finish(2)
    own_part(0, 0)
    own_part(1, 0)
    t.finish(3)
    own_part(0, 1)

    BLK = 64
    seg = rows // SEGS
    index = lax.broadcasted_iota(jnp.int32, (SEGS, LANES), 0)
    later = ctx + 1
    before = lax.max(ctx, 1) - 1

    def tail(g):
        return remote(
            prev.at[g, 0], prev.at[g, 1], ss.at[13 + g], rs.at[13 + g], dev(h, (later // 2) % 4, y, x, later % 2)
        )

    def project_rows(g):
        if g == 0:
            for p in range(HALVES):
                part(p).wait_recv()
        else:
            for s in range(3):
                part_b(s).wait_recv()

        @pl.loop(0, rows // BLK)
        def _(i):
            r = pl.ds(pl.multiple_of(i * BLK, BLK), BLK)
            total = acc[g, r, :] + precv[g, r, :].astype(F32)
            pf[g, pl.ds(pl.multiple_of(i * BLK + 8, 8), BLK), :] = total.astype(BF).astype(F32)

        prev[g, 0] = pf[g, pl.ds(rows - 8, 16), :].astype(BF)

        @pl.when(ctx < 7)
        def _():
            tail(g).start()

    def features(g):
        at = pl.ds(g * LANES, LANES)

        def some(i):
            feats = []
            for s in range(3):
                feat = None
                block = pf[g, pl.ds(pl.multiple_of(i * BLK, BLK), BLK + 8), pl.ds(s * LANES, LANES)]
                for k in range(3):
                    piece = block[8 - k : 8 - k + BLK]
                    term = taps[k, pl.ds(s, 1), at] * piece
                    feat = term if feat is None else feat + term
                feats.append(feat)
            r = pl.ds(pl.multiple_of(i * BLK, BLK), BLK)
            q_s[g, r, :] = feats[0]
            u_s[g, r, :] = feats[1] * feats[2]

        pl.loop(1, rows // BLK)(some)

        @pl.when(ctx > 0)
        def _():
            tail(g).wait_recv()
            pf[g, 0:8, :] = prev[g, 1].astype(F32)[8:16]

        @pl.when(ctx == 0)
        def _():
            pf[g, 0:8, :] = jnp.zeros((8, wide), F32)

        pl.loop(0, 1)(some)

    def rates(g):
        return [decay[pl.ds(r, 1), pl.ds(g * LANES, LANES)] for r in range(modes)]

    def state_copy(g, d, to, slot):
        return remote(ends.at[g], states.at[g, slot], es.at[g, d - 1], er.at[g, d - 1], to)

    def scan_ends(g):
        rate = rates(g)
        pole = [jnp.broadcast_to(jnp.exp(-d), (SEGS, LANES)) for d in rate]

        def grow(step, state):
            row = u_s[g, pl.ds(step, SEGS, stride=seg), :]
            return tuple(p * s + row for p, s in zip(pole, state))

        state = lax.fori_loop(0, seg, grow, tuple(jnp.zeros((SEGS, LANES), F32) for _ in range(modes)), unroll=2)
        for r in range(modes):
            value = state[r]
            for k in (1, 2, 4):
                moved = jnp.where(index >= k, pltpu.roll(value, k, 0), 0.0)
                value = value + jnp.exp(-(seg * k) * rate[r]) * moved
            ends[g, pl.ds(r, 1), :] = value[SEGS - 1 : SEGS]
            exc[g, r] = jnp.where(index >= 1, pltpu.roll(value, 1, 0), 0.0)
        for d in range(1, 8):
            @pl.when(ctx + d < 8)
            def _():
                to = ctx + d
                state_copy(g, d, dev(h, (to // 2) % 4, y, x, to % 2), ctx).start()

    def scan_out(g):
        for d in range(1, 8):
            @pl.when(ctx - d >= 0)
            def _():
                state_copy(g, d, sibling, (ctx - d + 8) % 8).wait_recv()

        group = jnp.exp(-float(rows) * decay[:, pl.ds(g * LANES, LANES)])
        coming = lax.fori_loop(
            0, ctx, lambda j, value: group * value + states[g, j], jnp.zeros((modes, LANES), F32)
        )
        rate = rates(g)
        pole = [jnp.broadcast_to(jnp.exp(-d), (SEGS, LANES)) for d in rate]
        weight = []
        state = []
        for r in range(modes):
            single = jnp.exp(-rate[r])
            scale = residue[pl.ds(r, 1), pl.ds(g * LANES, LANES)] * jnp.sqrt(1.0 - single * single)
            weight.append(jnp.broadcast_to(scale, (SEGS, LANES)))
            lead = jnp.exp(-rate[r] * (index * seg).astype(F32))
            state.append(exc[g, r] + lead * coming[r : r + 1])

        def emit(step, state):
            row = u_s[g, pl.ds(step, SEGS, stride=seg), :]
            state = tuple(p * s + row for p, s in zip(pole, state))
            terms = [w * s for w, s in zip(weight, state)]
            while len(terms) > 1:
                terms = [a + b for a, b in zip(terms[0::2], terms[1::2])]
            y_s[g, pl.ds(step, SEGS, stride=seg), :] = terms[0]
            return state

        lax.fori_loop(0, seg, emit, tuple(state), unroll=2)

        @pl.loop(0, rows // BLK)
        def _(i):
            r = pl.ds(pl.multiple_of(i * BLK, BLK), BLK)
            conv = y_s[g, r, :] + skip[:, pl.ds(g * LANES, LANES)] * u_s[g, r, :]
            gat[g, y, r, mine_h] = (q_s[g, r, :] * conv).astype(BF)

    mine_h = pl.ds(pl.multiple_of(h * LANES, LANES), LANES)
    other_h = pl.ds(pl.multiple_of((1 - h) * LANES, LANES), LANES)
    def swap(g, p, arriving):
        unit = gat.at[g, y, pl.ds(p * step, step), other_h if arriving else mine_h]
        return remote(unit, unit, xs.at[g, p], xr.at[g, p], opposite)

    def along(g, o, p, slot, arriving):
        way = 1 if slot % 2 == 0 else -1
        origin = 0 if slot < 2 else -way
        if arriving:
            origin = origin - way
        if slot < 2:
            r = pl.ds(p * step, step)
        else:
            r = pl.ds(p * step + (slot - 2) * (step // 2), step // 2)
        unit = gat.at[g, (y + origin + 4) % 4, r, mine_h if o == 0 else other_h]
        return remote(unit, unit, ps2.at[g, o * 2 + p, slot], gr.at[g, o, p, slot], dev(h, l, (y + way + 4) % 4, x, c))

    def send_gated(g, p):
        swap(g, p, False).start()
        for slot in (0, 1):
            along(g, 0, p, slot, False).start()

    def pass_swap(g, p):
        swap(g, p, True).wait_recv()
        for slot in (0, 1):
            along(g, 1, p, slot, False).start()

    def pass_along(g, o, p):
        for slot in (0, 1):
            along(g, o, p, slot, True).wait_recv()
            along(g, o, p, slot + 2, False).start()

    def have_gated(g, p):
        for o in range(2):
            for slot in (2, 3):
                along(g, o, p, slot, True).wait_recv()

    def output(g, to_x, p):
        r = pl.ds(p * step, step)
        total = jnp.zeros((step, chans), F32)
        for k in range(4):
            block = jnp.concatenate([wx[to_x, g, k], wx[to_x, g, 4 + k]], axis=0)
            total = total + jnp.dot(gat[g, k, r, :], block, preferred_element_type=F32)
        return total

    def result(d, p, arriving):
        r = pl.ds(p * step, step)
        return remote(
            osend.at[d - 1, r], orecv.at[d - 1, r], ps1.at[p, d - 1], orr.at[d - 1, p], dev(h, l, y, (x + d) % 4, c)
        )

    project_rows(0)
    own_part(1, 1)
    project_rows(1)
    features(0)
    scan_ends(0)
    features(1)
    scan_ends(1)
    t.wait_sends(2)
    t.wait_sends(3)
    for copy in o_loc:
        copy.wait()
    scan_out(0)
    send_gated(0, 0)
    scan_out(1)
    send_gated(1, 0)
    send_gated(0, 1)
    send_gated(1, 1)
    pass_along(0, 0, 0)
    pass_along(1, 0, 0)
    pass_along(0, 0, 1)
    pass_swap(0, 0)
    pass_along(1, 0, 1)
    pass_swap(1, 0)
    pass_swap(0, 1)
    pass_swap(1, 1)
    for d in (1, 3, 2):
        o_send(d, True).wait_recv()
        o_fwd(d, False).start()
    pass_along(0, 1, 0)
    pass_along(1, 1, 0)
    pass_along(0, 1, 1)
    pass_along(1, 1, 1)
    for d in (1, 3, 2):
        o_fwd(d, True).wait_recv()
    have_gated(0, 0)
    have_gated(1, 0)

    def send_results(p):
        r = pl.ds(p * step, step)
        for d in (2, 1, 3):
            to_x = (x + d) % 4
            osend[d - 1, r, :] = (output(0, to_x, p) + output(1, to_x, p)).astype(BF)
            result(d, p, False).start()

    send_results(0)
    have_gated(0, 1)
    have_gated(1, 1)
    send_results(1)
    for p in range(HALVES):
        acc2[pl.ds(p * step, step), :] = output(0, x, p) + output(1, x, p)
    for p in range(HALVES):
        r = pl.ds(p * step, step)
        for d in (2, 1, 3):
            result(d, p, True).wait_recv()
        out[r, :] = (
            acc2[r, :] + orecv[0, r, :].astype(F32) + orecv[1, r, :].astype(F32) + orecv[2, r, :].astype(F32)
        ).astype(BF)

    @pl.when(foreign_type)
    def _():
        for p in range(HALVES):
            token_copy(0, p).wait_send()
            token_copy(1, p).wait_send()

    @pl.when(jnp.logical_not(foreign_type))
    def _():
        for p in range(HALVES):
            token_copy(2, p).wait_send()

    for g in range(groups):
        w_sib(g, mine_q).wait_send()
        for p in range(HALVES):
            swap(g, p, False).wait_send()
            for o in range(2):
                for slot in range(4):
                    along(g, o, p, slot, False).wait_send()

        @pl.when(ctx < 7)
        def _():
            tail(g).wait_send()

        for d in range(1, 8):
            @pl.when(ctx + d < 8)
            def _():
                state_copy(g, d, sibling, ctx).wait_send()

    w_near(0, mine_q).wait_send()
    w_fwd(0, near_q).wait_send()
    for p in range(HALVES):
        part(p).wait_send()
    for s in range(3):
        w_near_b(s, mine_q).wait_send()
        w_fwd_b(s, near_q).wait_send()
        part_b(s).wait_send()
    for d in (1, 3, 2):
        o_send(d, False).wait_send()
        o_fwd(d, False).wait_send()
        for p in range(HALVES):
            result(d, p, False).wait_send()

def body(tokens, w_in, short_taps, decay_rate, residue, skip_gain, w_out):
    rows, chans = tokens.shape
    depth = w_in.shape[0]
    modes = decay_rate.shape[1]
    groups = chans // LANES
    vmem = pl.BlockSpec(memory_space=pltpu.VMEM)
    any_ = pl.BlockSpec(memory_space=pl.ANY)
    dma = pltpu.SemaphoreType.DMA
    return pl.pallas_call(
        kernel,
        out_shape=jax.ShapeDtypeStruct((rows, chans), BF),
        in_specs=[vmem, any_, vmem, vmem, vmem, vmem, any_],
        out_specs=vmem,
        scratch_shapes=[
            pltpu.VMEM((2, 16, rows, chans), BF),
            pltpu.VMEM((4, groups, 3, depth, LANES), BF),
            pltpu.VMEM((4, groups, 8, LANES, chans), BF),
            pltpu.VMEM((groups, 4, rows, 2 * LANES), BF),
            pltpu.VMEM((groups, rows, 3 * LANES), BF),
            pltpu.VMEM((groups, rows, 3 * LANES), BF),
            pltpu.VMEM((groups, rows, 3 * LANES), F32),
            pltpu.VMEM((rows, chans), F32),
            pltpu.VMEM((3, rows, chans), BF),
            pltpu.VMEM((3, rows, chans), BF),
            pltpu.VMEM((groups, rows + 8, 3 * LANES), F32),
            pltpu.VMEM((groups, 2, 16, 3 * LANES), BF),
            pltpu.VMEM((groups, rows, LANES), F32),
            pltpu.VMEM((groups, rows, LANES), F32),
            pltpu.VMEM((groups, rows, LANES), F32),
            pltpu.VMEM((groups, modes, SEGS, LANES), F32),
            pltpu.VMEM((groups, modes, LANES), F32),
            pltpu.VMEM((groups, 8, modes, LANES), F32),
            dma((2, 3)),
            dma((2 * HALVES, 3)),
            dma((2, 4, 4)),
            dma((2 * HALVES, 4, 4)),
            dma((21,)),
            dma((21,)),
            dma((9,)),
            dma((groups, 7)),
            dma((groups, 7)),
            dma((2, groups)),
            dma((2, groups)),
            dma((groups, 2, HALVES, 4)),
            dma((groups, HALVES)),
            dma((groups, HALVES)),
            dma((3, HALVES)),
            dma((3, HALVES)),
            dma((2, HALVES)),
            dma((HALVES,)),
            dma((HALVES,)),
            dma((3, 3)),
            dma((3, 3)),
        ],
        compiler_params=pltpu.CompilerParams(collective_id=0, has_side_effects=True, vmem_limit_bytes=56 << 20),
        name="hyena",
    )(
        tokens, jnp.transpose(w_in, (1, 0, 2)), short_taps, decay_rate.T, residue.T,
        skip_gain.reshape(1, chans), w_out.reshape(8, 4, groups, LANES, chans),
    )


def solution(mesh):
    in_specs = (
        P("ctx", "tp"),
        P("ctx", None, "tp"),
        P(None, None, "tp"),
        P("tp", None),
        P("tp", None),
        P("tp"),
        P(None, "tp"),
    )
    return jax.shard_map(body, mesh=mesh, in_specs=in_specs, out_specs=P("ctx", "tp"), check_vma=False)
```
